512 devices in a mesh: dp: 4 (over y), row: 4 (over x), col: 32 (over z, core).
Axes of the slice: x: 4, y: 4, z: 16, core: 2. Of those that a mesh axis runs over, the one named last changes fastest.
Arguments:
- inputs: bfloat16 [2048, 6144], P(('dp', 'row'), 'col'), may hold values from -6 to 6
- out_grad: bfloat16 [2048, 6144], P(('dp', 'row'), 'col'), may hold values from -6 to 6
- up_blocks: bfloat16 [4, 32, 16, 128, 128], P('row', 'col'), may hold values from -0.25 to 0.25
- up_index: int32 [4, 32, 16], P('row', 'col'), may hold values from -1 to 71, as said below
- down_blocks: bfloat16 [4, 32, 16, 128, 128], P('row', 'col'), may hold values from -0.125 to 0.125
- down_index: int32 [4, 32, 16], P('row', 'col'), may hold values from -1 to 71, as said below
Outputs:
- in_grad: bfloat16 [2048, 6144], P(('dp', 'row'), 'col')
- up_grad: bfloat16 [4, 32, 16, 128, 128], P('row', 'col', 'dp')
- down_grad: bfloat16 [4, 32, 16, 128, 128], P('row', 'col', 'dp')
The draws below stay inside these ranges and needn't reach their ends.
Inputs may be any that keep to these rules, and one draw needn't show every extreme that they name: `up_index`: in each shard the indices of the first slots are distinct positions of 0 to 71 and all later slots are -1. Some shard fills all 16 slots; the shards of one column slab together hold at most 46 kept blocks, and some column slab holds exactly 46. `down_index`: as for up_index, with positions of 0 to 71; some shard fills all 16 slots and some column slab holds exactly 46 kept blocks.
All inputs are finite; a program needn't handle non-finite values.
Results may differ from the reference program's by a relative error of at most 0.022.
Values may be sent and summed in bfloat16 or wider, within the bound.
A program may use at most 64 MiB of HBM per device.

```python
import math
import jax
import jax.numpy as jnp
from jax import lax

D = 6144
H = 24576
BLK = 128
CAP = 16
BASE_MOST = 10
TOKENS = 2048
KR = 12
NC = 6
N_ROW = 4
N_COL = 32


def shard_lists(key):
    places = KR * NC
    key_base, key_row, key_col, key_order = jax.random.split(key, 4)
    base = jax.random.randint(key_base, (N_ROW, N_COL), max(1, BASE_MOST - 6), BASE_MOST + 1)
    full_row = jax.random.randint(key_row, (), 0, N_ROW)
    full_col = jax.random.randint(key_col, (), 0, N_COL)
    rows = jnp.arange(N_ROW, dtype=jnp.int32)[:, None]
    cols = jnp.arange(N_COL, dtype=jnp.int32)[None, :]
    counts = jnp.where(cols == full_col, jnp.where(rows == full_row, CAP, BASE_MOST), base)
    scores = jax.random.randint(key_order, (N_ROW, N_COL, places), 0, 65536) * places + jnp.arange(places, dtype=jnp.int32)
    order = jnp.argsort(scores, axis=-1, stable=True).astype(jnp.int32)[:, :, :CAP]
    slot = jnp.arange(CAP, dtype=jnp.int32)
    return jnp.where(slot[None, None, :] < counts[:, :, None], order, -1).astype(jnp.int32)


def draw_up_index(key, part):
    key = jax.random.fold_in(key, 11)
    return shard_lists(key)


def draw_down_index(key, part):
    key = jax.random.fold_in(key, 23)
    return shard_lists(key)


def steps_of(own_key, dims, shards, low, largest):
    def one(dim, parts):
        steps = jax.random.uniform(jax.random.fold_in(jax.random.fold_in(own_key, 6), dim), (parts,), jnp.float32, low / len(shards), largest / len(shards))
        return jnp.repeat(jnp.exp(steps), dims[dim] // parts).reshape((-1,) + (1,) * (len(dims) - dim - 1))

    loudness = one(*shards[0])
    for cut in shards[1:]:
        loudness = loudness * one(*cut)
    return loudness


def scatter_about(rng, dims, deviation, most, cuts=(), held_as=jnp.bfloat16):
    entries = jax.random.normal(rng, dims, jnp.float32) * deviation
    if len(cuts) > 0:
        entries = steps_of(rng, dims, cuts, -0.22, 0.18) * entries
    return jnp.clip(entries, min=-most, max=most).astype(held_as)


def setup_inputs(seed: int = 0) -> dict:
    arg_keys = jax.random.split(jax.random.key(seed), 7)
    return {
        "inputs": scatter_about(arg_keys[0], (TOKENS, D), 1.0, 6.0, ((0, 16), (1, 32))),
        "out_grad": scatter_about(arg_keys[1], (TOKENS, D), 1.0, 6.0, ((0, 16), (1, 32))),
        "up_blocks": scatter_about(arg_keys[2], (N_ROW, N_COL, CAP, BLK, BLK), (D // 10) ** -0.5, 0.25, ((0, 4), (1, 32))),
        "up_index": draw_up_index(jax.random.fold_in(arg_keys[6], 71), 0),
        "down_blocks": scatter_about(arg_keys[4], (N_ROW, N_COL, CAP, BLK, BLK), (H // 10) ** -0.5, 0.125, ((0, 4), (1, 32))),
        "down_index": draw_down_index(jax.random.fold_in(arg_keys[6], 71), 0),
    }


root_two_pi = math.sqrt(2.0 / math.pi)

def gelu_parts(value):
    inner = root_two_pi * (value + 0.044715 * value * value * value)
    tanh_inner = jnp.tanh(inner)
    result = 0.5 * value * (1.0 + tanh_inner)
    slope = 0.5 * (1.0 + tanh_inner) + 0.5 * value * (1.0 - tanh_inner * tanh_inner) * root_two_pi * (1.0 + 3.0 * 0.044715 * value * value)
    return (result, slope)

def reference(inputs, out_grad, up_blocks, up_index, down_blocks, down_index):
    highest = lax.Precision.HIGHEST
    block_rows = D // BLK
    scale = 1.0 / math.sqrt(TOKENS)
    input_tiles = inputs.reshape(TOKENS, block_rows, BLK)
    cotan_tiles = out_grad.reshape(TOKENS, block_rows, BLK)
    owners = jnp.arange(N_ROW, dtype=jnp.int32)[:, None]
    slots = N_ROW * CAP

    def slab(input_total, items):
        up_part, up_slots, down_part, down_slots = items
        up_valid = up_slots >= 0
        up_place = jnp.maximum(up_slots, 0)
        up_row = (owners * KR + up_place // NC).reshape(slots)
        up_col = (up_place % NC).reshape(slots)
        up_mask = up_valid.reshape(slots).astype(jnp.float32)
        up_matrix = up_part.reshape(slots, BLK, BLK).astype(jnp.float32) * up_mask[:, None, None]
        down_valid = down_slots >= 0
        down_place = jnp.maximum(down_slots, 0)
        down_row = (down_place // KR).reshape(slots)
        down_col = (owners * KR + down_place % KR).reshape(slots)
        down_mask = down_valid.reshape(slots).astype(jnp.float32)
        down_matrix = down_part.reshape(slots, BLK, BLK).astype(jnp.float32) * down_mask[:, None, None]
        local_cols = jnp.arange(NC, dtype=jnp.int32)
        up_onehot = (up_col[:, None] == local_cols[None, :]).astype(jnp.float32)
        down_onehot = (down_row[:, None] == local_cols[None, :]).astype(jnp.float32)
        input_taken = jnp.take(input_tiles, up_row, axis=1).astype(jnp.float32)
        product = jnp.einsum('tsk,skn->tsn', input_taken, up_matrix, precision=highest)
        pre_act = jnp.einsum('tsn,sc->tcn', product, up_onehot, precision=highest)
        act_value, slope = gelu_parts(pre_act)
        act_low = act_value.astype(jnp.bfloat16)
        cotan_taken = jnp.take(cotan_tiles, down_col, axis=1).astype(jnp.float32)
        act_terms = jnp.einsum('tsj,sij->tsi', cotan_taken, down_matrix, precision=highest)
        act_grad = jnp.einsum('tsi,sc->tci', act_terms, down_onehot, precision=highest)
        pre_grad = (act_grad * slope).astype(jnp.bfloat16)
        pre_taken = jnp.take(pre_grad, up_col, axis=1).astype(jnp.float32)
        input_terms = jnp.einsum('tsn,skn->tsk', pre_taken, up_matrix, precision=highest)
        row_onehot = (up_row[:, None] == jnp.arange(block_rows, dtype=jnp.int32)[None, :]).astype(jnp.float32)
        input_slab = jnp.einsum('tsk,sb->tbk', input_terms, row_onehot, precision=highest)
        slab_low = lax.optimization_barrier(input_slab.astype(jnp.bfloat16))
        input_total = input_total + slab_low.astype(jnp.float32)
        grad_upper = jnp.einsum('tsk,tsn->skn', input_taken, pre_taken, precision=highest) * scale * up_mask[:, None, None]
        act_taken = jnp.take(act_low, down_row, axis=1).astype(jnp.float32)
        grad_lower = jnp.einsum('tsi,tsj->sij', act_taken, cotan_taken, precision=highest) * scale * down_mask[:, None, None]
        grad_upper = grad_upper.reshape(N_ROW, CAP, BLK, BLK).astype(jnp.bfloat16)
        grad_lower = grad_lower.reshape(N_ROW, CAP, BLK, BLK).astype(jnp.bfloat16)
        return (input_total, (grad_upper, grad_lower))
    items = (jnp.swapaxes(up_blocks, 0, 1), jnp.swapaxes(up_index, 0, 1), jnp.swapaxes(down_blocks, 0, 1), jnp.swapaxes(down_index, 0, 1))
    begin = jnp.zeros((TOKENS, block_rows, BLK), jnp.float32)
    input_total, (grads_upper, grads_lower) = lax.scan(slab, begin, items)
    in_grad = input_total.reshape(TOKENS, D).astype(jnp.bfloat16)
    up_grad = jnp.swapaxes(grads_upper, 0, 1)
    down_grad = jnp.swapaxes(grads_lower, 0, 1)
    return (in_grad, up_grad, down_grad)
```

```python
import functools
import math

import jax
import jax.numpy as jnp
from jax import lax
from jax.experimental import pallas as pl
from jax.experimental.pallas import tpu as pltpu
from jax.sharding import PartitionSpec as P

MESH = pl.DeviceIdType.MESH
BF = jnp.bfloat16
F32 = jnp.float32
ROOT = math.sqrt(2.0 / math.pi)

BLK = 128
CAP = 16
KR = 12
NC = 6
HALF = 64
PB = 3

DIRECT = 8


def tree(count, twos):
    strides = [2] * twos + [1] * (count - 2 * twos)
    marks = [0]
    for step in strides:
        marks.append(marks[-1] + step)
    return strides, marks


def gelu_parts(value):
    inner = ROOT * (value + 0.044715 * value * value * value)
    tanh_inner = jnp.tanh(inner)
    result = 0.5 * value * (1.0 + tanh_inner)
    slope = 0.5 * (1.0 + tanh_inner) + 0.5 * value * (
        1.0 - tanh_inner * tanh_inner
    ) * ROOT * (1.0 + 3.0 * 0.044715 * value * value)
    return result, slope


def nt_dot(a, b):
    return lax.dot_general(a, b, (((1,), (1,)), ((), ())), preferred_element_type=F32)


def kernel(
    sizes,
    x_ref, g_ref, wu_hbm, ui_ref, wd_hbm, di_ref,
    in_ref, up_ref, down_ref,
    xb, gb, wub, wdb, meta_v, meta_s, half_in, p_ref, a_ref, pg_ref, act_t, pg_t,
    dwd, dwu, sdown, sup, rdown, rup, rdown2, rup2,
    own, mine, theirs, ring_out, ring_leaf, ring_bone, fin, fin_in,
    half_s, half_r, meta_ss, meta_r, meta_l, wsend, whelp, wrecv, wlocal,
    ag_s, ag_r, sib_s, sib_r,
    d1_s, d1_r, u1_s, u1_r, d2_s, d2_r, u2_s, u2_r,
    part_s, part_r, ring_s, leaf_r, bone_r, fin_s, fin_r,
):
    nd, nr, nz = sizes
    scale = 1.0 / math.sqrt(nd * nr * 2 * HALF)
    xg, wb = (xb, gb), (wub, wdb)
    d, r, c = lax.axis_index("dp"), lax.axis_index("row"), lax.axis_index("col")
    z, h = c // 2, c % 2
    o = 1 - h
    sibling = (d, r, z * 2 + o)
    n_of = {1: nz // 2, -1: nz // 2 - 1}

    def xpeer(k):
        return (d, lax.rem(r + k, nr), c)

    def ypeer(k):
        return (lax.rem(d + k, nd), r, c)

    def zpeer(k):
        return (d, r, lax.rem(z + nz + k, nz) * 2 + h)

    def send(src, dst, ss, rs, to):
        copy = pltpu.make_async_remote_copy(
            src_ref=src, dst_ref=dst, send_sem=ss, recv_sem=rs, device_id=to, device_id_type=MESH
        )
        copy.start()

    def drain(ref, sem):
        pltpu.make_async_copy(ref, ref, sem).wait()

    partners = [sibling] + [zpeer(k) for k in (1, -1, 2, -2)]
    partners += [xpeer(k) for k in range(1, nr)] + [ypeer(k) for k in range(1, nd)]
    barrier = pltpu.get_barrier_semaphore()
    for to in partners:
        pl.semaphore_signal(barrier, inc=1, device_id=to, device_id_type=MESH)
    pl.semaphore_wait(barrier, len(partners))

    mine_rows = pl.ds(pl.multiple_of(h * HALF, HALF), HALF)
    their_rows = pl.ds(pl.multiple_of(o * HALF, HALF), HALF)
    srcs = (x_ref, g_ref)
    for a in range(2):
        send(srcs[a].at[their_rows], half_in.at[a], half_s.at[a], half_r.at[a], sibling)

    lane = lax.broadcasted_iota(jnp.int32, (8, BLK), 1)
    line = lax.broadcasted_iota(jnp.int32, (8, BLK), 0)
    table = jnp.where(line >= 6, nr * CAP, 0)
    for s in range(CAP):
        up = ui_ref[0, 0, s]
        down = di_ref[0, 0, s]
        up_ok, down_ok = up >= 0, down >= 0
        up_p, down_p = jnp.maximum(up, 0), jnp.maximum(down, 0)
        entries = (
            r * KR + up_p // NC, up_p % NC, up_ok.astype(jnp.int32),
            down_p // KR, r * KR + down_p % KR, down_ok.astype(jnp.int32),
        )
        for i, entry in enumerate(entries):
            table = jnp.where((line == i) & (lane == s), entry, table)
        table = jnp.where((line == 6) & (lane == up), r * CAP + s, table)
        table = jnp.where((line == 7) & (lane == down), r * CAP + s, table)
    meta_v[r] = table
    for k in range(1, nr):
        send(meta_v.at[r], meta_v.at[r], meta_ss.at[k], meta_r.at[k], xpeer(k))

    for a in range(2):
        drain(half_in.at[a], half_r.at[a])
        kept = srcs[a][mine_rows, :]
        other = half_in[a]

        def place(low, high, a=a):
            whole = jnp.concatenate([low, high], axis=1)
            for i in range(PB):
                xg[a][PB * z + i, mine_rows, :] = whole[:, i * BLK:(i + 1) * BLK]

        @pl.when(h == 0)
        def _(kept=kept, other=other, place=place):
            place(kept, other)

        @pl.when(h == 1)
        def _(kept=kept, other=other, place=place):
            place(other, kept)

    def piece(a, k, rows=mine_rows):
        where = lax.rem(z + nz + k, nz)
        return xg[a].at[pl.ds(PB * where, PB), rows, :]

    def share(a, k):
        send(piece(a, k), piece(a, k), sib_s.at[a], sib_r.at[a], sibling)

    def gather_send(a, way, at, hop):
        ref = piece(a, -way * at)
        side = 0 if way == 1 else 1
        send(ref, ref, ag_s.at[a], ag_r.at[a, side, at + hop - 1], zpeer(way * hop))

    def gather_wait(a, way, at):
        side = 0 if way == 1 else 1
        drain(piece(a, -way * at), ag_r.at[a, side, at - 1])

    trees = {way: tree(n_of[way], n_of[way] // 2) for way in (1, -1)}

    def gather_step(a, way, j):
        strides, marks = trees[way]
        if j > len(strides):
            return
        at = marks[j]
        if j > 0:
            gather_wait(a, way, at)
        if j < len(strides):
            gather_send(a, way, at, strides[j])
            if strides[j] == 2:
                gather_send(a, way, at, 1)
        if j > 0:
            share(a, -way * at)
            if strides[j - 1] == 2:
                gather_wait(a, way, at - 1)
                share(a, -way * (at - 1))

    for a in range(2):
        for way in (1, -1):
            gather_step(a, way, 0)
        share(a, 0)

    srcw = (wu_hbm.at[0, 0], wd_hbm.at[0, 0])
    per = (CAP - DIRECT) // nd
    for a in range(2):
        for k in range(1, nr):
            send(
                srcw[a].at[pl.ds(per * d, per)], wb[a].at[pl.ds(CAP * r + per * d, per)],
                wsend.at[a], whelp.at[a, k], xpeer(k),
            )
    for a in range(2):
        for k in range(1, nr):
            send(
                srcw[a].at[pl.ds(CAP - DIRECT, DIRECT)],
                wb[a].at[pl.ds(CAP * r + CAP - DIRECT, DIRECT)],
                wsend.at[a], wrecv.at[a], xpeer(k),
            )
    locals_ = [
        pltpu.make_async_copy(srcw[a], wb[a].at[pl.ds(CAP * r, CAP)], wlocal.at[a]) for a in range(2)
    ]
    for copy in locals_:
        copy.start()
    for a in range(2):
        wb[a][nr * CAP] = jnp.zeros((BLK, BLK), BF)

    def help_on(a):
        for k in range(1, nr):
            src = lax.rem(r + nr - k, nr)
            ref = wb[a].at[pl.ds(CAP * src + per * d, per)]
            drain(ref, whelp.at[a, k])
            for ky in range(1, nd):
                send(ref, ref, wsend.at[a], wrecv.at[a], ypeer(ky))

    longest = max(len(trees[way][0]) for way in (1, -1))
    for j in range(1, longest + 1):
        for a in range(2):
            for way in (1, -1):
                gather_step(a, way, j)
        if j <= 2:
            help_on(j - 1)

    for k in range(1, nr):
        src = lax.rem(r + nr - k, nr)
        drain(meta_v.at[src], meta_r.at[k])
    to_smem = pltpu.make_async_copy(meta_v, meta_s, meta_l)
    to_smem.start()
    to_smem.wait()

    for a in range(2):
        drain(xg[a].at[:, pl.ds(0, HALF), :], sib_r.at[a])
    def weights_here(a):
        locals_[a].wait()
        got = (nr - 1) * DIRECT + (nr - 1) * (nd - 1) * per
        drain(wb[a].at[pl.ds(0, got)], wrecv.at[a])

    weights_here(0)
    step_rows = 4
    steps = nr * KR // step_rows
    per_owner = KR // step_rows
    p_ref[...] = jnp.zeros_like(p_ref)
    a_ref[...] = jnp.zeros_like(a_ref)

    @pl.loop(0, steps)
    def _(t):
        owner, base = t // per_owner, (t % per_owner) * step_rows
        left = jnp.concatenate([xb[step_rows * t + i] for i in range(step_rows)], axis=1)
        right = jnp.concatenate(
            [
                jnp.concatenate(
                    [wub[meta_s[owner, 6, (base + i) * NC + j]] for j in range(NC)], axis=1
                )
                for i in range(step_rows)
            ],
            axis=0,
        )
        p_ref[...] += jnp.dot(left, right, preferred_element_type=F32)

    act, slope = gelu_parts(p_ref[...])
    act_low = act.astype(BF)
    p_ref[...] = slope
    for i in range(NC):
        act_t[i] = act_low[:, i * BLK:(i + 1) * BLK].T

    def down_terms(owner):
        @pl.loop(0, CAP // 4)
        def _(t):
            for u in range(4):
                s = 4 * t + u
                i, j = meta_s[owner, 3, s], meta_s[owner, 4, s]
                keep = meta_s[owner, 5, s].astype(F32) * scale
                term = jnp.dot(act_t[i], gb[j], preferred_element_type=F32)
                dwd[owner, s] = (term * keep).astype(BF)

    for k in (2, 1, 3):
        owner = lax.rem(r + k, nr)
        down_terms(owner)
        send(dwd.at[owner], rdown.at[k - 1], d1_s, d1_r.at[k - 1], xpeer(k))
    down_terms(r)

    weights_here(1)

    @pl.loop(0, steps)
    def _(t):
        owner, base = t // per_owner, (t % per_owner) * step_rows
        left = jnp.concatenate([gb[step_rows * t + i] for i in range(step_rows)], axis=1)
        right = jnp.concatenate(
            [
                jnp.concatenate(
                    [wdb[meta_s[owner, 7, i * KR + base + j]] for j in range(step_rows)], axis=1
                )
                for i in range(NC)
            ],
            axis=0,
        )
        a_ref[...] += nt_dot(left, right)

    pre_grad = (a_ref[...] * p_ref[...]).astype(BF)
    for i in range(NC):
        pg_t[i] = pre_grad[:, i * BLK:(i + 1) * BLK].T
    pg_ref[0:HALF, :] = pre_grad[0:HALF, :]
    pg_ref[HALF:2 * HALF, :] = pre_grad[HALF:2 * HALF, :]
    pg_ordered = jnp.concatenate([pg_ref[mine_rows, :], pg_ref[their_rows, :]], axis=0)
    pg_ref[...] = pg_ordered

    def up_terms(owner_y):
        @pl.loop(0, nr)
        def _(owner):
            for u in range(CAP // nd):
                s = (CAP // nd) * owner_y + u
                k, j = meta_s[owner, 0, s], meta_s[owner, 1, s]
                keep = meta_s[owner, 2, s].astype(F32) * scale
                term = jnp.dot(pg_t[j], xb[k], preferred_element_type=F32)
                dwu[owner, s] = (term * keep).astype(BF)

    share_y = CAP // nd
    for k in (2, 1, 3):
        owner_y = lax.rem(d + k, nd)
        up_terms(owner_y)
        send(
            dwu.at[:, pl.ds(share_y * owner_y, share_y)], rup.at[k - 1], u1_s, u1_r.at[k - 1], ypeer(k)
        )
    up_terms(d)

    def partial_piece(index, k):
        where = lax.rem(z + nz + k, nz)
        owner = where // (KR // PB)
        base = (where % (KR // PB)) * PB
        right = jnp.concatenate(
            [
                jnp.concatenate(
                    [wub[meta_s[owner, 6, (base + i) * NC + j]] for j in range(NC)], axis=1
                )
                for i in range(PB)
            ],
            axis=0,
        )
        both = nt_dot(pg_ref[...], right)
        for i in range(PB):
            own[index, i] = both[0:HALF, i * BLK:(i + 1) * BLK]
            mine[index, i] = both[HALF:2 * HALF, i * BLK:(i + 1) * BLK].astype(BF)
        send(mine.at[index], theirs.at[index], part_s, part_r.at[index], sibling)

    n_right, n_left = n_of[1], n_of[-1]

    def index_of(way, at):
        return at - 1 if way == 1 else n_right + at - 1

    order = []
    for at in range(n_right, 0, -1):
        order.append((1, at))
        if at <= n_left:
            order.append((-1, at))
    for way, at in order:
        partial_piece(index_of(way, at), way * at)
    partial_piece(nz - 1, 0)

    def summed(index, extra):
        drain(theirs.at[index], part_r.at[index])
        total = own[index] + theirs[index].astype(F32)
        for ref in extra:
            total = total + ref[...].astype(F32)
        return total

    def incoming(way, at):
        strides, marks = trees[way]
        side = 0 if way == 1 else 1
        refs = []
        j = marks.index(at)
        if j < len(strides):
            if strides[j] == 2:
                refs.append((ring_leaf.at[side, at], leaf_r.at[side, at]))
            refs.append((ring_bone.at[side, at], bone_r.at[side, at]))
        return refs

    def ring_step(way, at):
        strides, marks = trees[way]
        side = 0 if way == 1 else 1
        index = index_of(way, at)
        if at in marks:
            refs = incoming(way, at)
            for ref, sem in refs:
                drain(ref, sem)
            total = summed(index, [ref for ref, _ in refs])
            hop = strides[marks.index(at) - 1]
            ring_out[index] = total.astype(BF)
            send(
                ring_out.at[index], ring_bone.at[side, at - hop], ring_s, bone_r.at[side, at - hop],
                zpeer(way * hop),
            )
        else:
            ring_out[index] = summed(index, []).astype(BF)
            send(
                ring_out.at[index], ring_leaf.at[side, at - 1], ring_s, leaf_r.at[side, at - 1],
                zpeer(way * 1),
            )

    def waits(way, at):
        marks = trees[way][1]
        return at in marks[:-1]

    for way, at in order:
        if not waits(way, at):
            ring_step(way, at)
    for way, at in order:
        if waits(way, at):
            ring_step(way, at)

    refs = incoming(1, 0) + incoming(-1, 0)
    for ref, sem in refs:
        drain(ref, sem)
    total = summed(nz - 1, [ref for ref, _ in refs])
    flat = jnp.concatenate([total[i] for i in range(PB)], axis=1).astype(BF)
    width = x_ref.shape[1]
    fin[0] = flat[:, 0:width]
    fin[1] = flat[:, width:2 * width]
    send(fin.at[o], fin_in, fin_s, fin_r, sibling)
    in_ref[mine_rows, :] = fin[h]
    drain(fin_in, fin_r)
    in_ref[their_rows, :] = fin_in[...]

    for k in range(1, nr):
        drain(rdown.at[k - 1], d1_r.at[k - 1])

    @pl.loop(0, CAP)
    def _(s):
        total = dwd[r, s].astype(F32)
        for k in range(nr - 1):
            total += rdown[k, s].astype(F32)
        sdown[s] = total.astype(BF)

    for k in (2, 1, 3):
        owner_y = lax.rem(d + k, nd)
        send(
            sdown.at[pl.ds(share_y * owner_y, share_y)], rdown2.at[k - 1], d2_s, d2_r.at[k - 1], ypeer(k)
        )

    for k in range(1, nd):
        drain(rup.at[k - 1], u1_r.at[k - 1])

    @pl.loop(0, nr)
    def _(owner):
        for u in range(share_y):
            total = dwu[owner, share_y * d + u].astype(F32)
            for k in range(nd - 1):
                total += rup[k, owner, u].astype(F32)
            sup[owner, u] = total.astype(BF)

    for k in (2, 1, 3):
        owner = lax.rem(r + k, nr)
        send(sup.at[owner], rup2.at[k - 1], u2_s, u2_r.at[k - 1], xpeer(k))

    for k in range(1, nd):
        drain(rdown2.at[k - 1], d2_r.at[k - 1])
    for u in range(share_y):
        total = sdown[share_y * d + u].astype(F32)
        for k in range(nd - 1):
            total += rdown2[k, u].astype(F32)
        down_ref[0, 0, u] = total.astype(BF)

    for k in range(1, nr):
        drain(rup2.at[k - 1], u2_r.at[k - 1])
    for u in range(share_y):
        total = sup[r, u].astype(F32)
        for k in range(nr - 1):
            total += rup2[k, u].astype(F32)
        up_ref[0, 0, u] = total.T.astype(BF)

    for a in range(2):
        drain(half_in.at[a], half_s.at[a])
        drain(xg[a].at[pl.ds(0, PB * (nz - 1)), pl.ds(0, HALF), :], ag_s.at[a])
        drain(xg[a].at[:, pl.ds(0, HALF), :], sib_s.at[a])
        gone = (nr - 1) * (per + DIRECT) + (nr - 1) * (nd - 1) * per
        drain(wb[a].at[pl.ds(0, gone)], wsend.at[a])
    for k in range(1, nr):
        drain(meta_v.at[r], meta_ss.at[k])
    drain(rdown, d1_s)
    drain(rup, u1_s)
    drain(rdown2, d2_s)
    drain(rup2, u2_s)
    drain(mine, part_s)
    drain(ring_out, ring_s)
    drain(fin_in, fin_s)


def solution(mesh):
    nd, nr, nc = mesh.shape["dp"], mesh.shape["row"], mesh.shape["col"]
    nz = nc // 2
    DMA = pltpu.SemaphoreType.DMA
    VMEM = pltpu.VMEM

    def body(inputs, out_grad, up_blocks, up_index, down_blocks, down_index):
        tokens, width = inputs.shape
        blocks = nr * KR
        hidden = NC * BLK
        share = CAP // nd
        vmem = pl.BlockSpec(memory_space=pltpu.VMEM)
        smem = pl.BlockSpec(memory_space=pltpu.SMEM)
        hbm = pl.BlockSpec(memory_space=pl.ANY)
        scratch = [
            VMEM((blocks, tokens, BLK), BF),
            VMEM((blocks, tokens, BLK), BF),
            VMEM((nr * CAP + 1, BLK, BLK), BF),
            VMEM((nr * CAP + 1, BLK, BLK), BF),
            VMEM((nr, 8, BLK), jnp.int32),
            pltpu.SMEM((nr, 8, BLK), jnp.int32),
            VMEM((2, HALF, width), BF),
            VMEM((tokens, hidden), F32),
            VMEM((tokens, hidden), F32),
            VMEM((tokens, hidden), BF),
            VMEM((NC, BLK, tokens), BF),
            VMEM((NC, BLK, tokens), BF),
            VMEM((nr, CAP, BLK, BLK), BF),
            VMEM((nr, CAP, BLK, BLK), BF),
            VMEM((CAP, BLK, BLK), BF),
            VMEM((nr, share, BLK, BLK), BF),
            VMEM((nr - 1, CAP, BLK, BLK), BF),
            VMEM((nd - 1, nr, share, BLK, BLK), BF),
            VMEM((nd - 1, share, BLK, BLK), BF),
            VMEM((nr - 1, share, BLK, BLK), BF),
            VMEM((nz, PB, HALF, BLK), F32),
            VMEM((nz, PB, HALF, BLK), BF),
            VMEM((nz, PB, HALF, BLK), BF),
            VMEM((nz - 1, PB, HALF, BLK), BF),
            VMEM((2, nz // 2, PB, HALF, BLK), BF),
            VMEM((2, nz // 2, PB, HALF, BLK), BF),
            VMEM((2, HALF, width), BF),
            VMEM((HALF, width), BF),
            DMA((2,)), DMA((2,)),
            DMA((nr,)), DMA((nr,)), DMA,
            DMA((2,)), DMA((2, nr)), DMA((2,)), DMA((2,)),
            DMA((2,)), DMA((2, 2, nz // 2)),
            DMA((2,)), DMA((2,)),
            DMA, DMA((nr - 1,)), DMA, DMA((nd - 1,)),
            DMA, DMA((nd - 1,)), DMA, DMA((nr - 1,)),
            DMA, DMA((nz,)),
            DMA, DMA((2, nz // 2)), DMA((2, nz // 2)),
            DMA, DMA,
        ]
        return pl.pallas_call(
            functools.partial(kernel, (nd, nr, nz)),
            out_shape=(
                jax.ShapeDtypeStruct((tokens, width), BF),
                jax.ShapeDtypeStruct((1, 1, share, BLK, BLK), BF),
                jax.ShapeDtypeStruct((1, 1, share, BLK, BLK), BF),
            ),
            in_specs=[vmem, vmem, hbm, smem, hbm, smem],
            out_specs=(vmem, vmem, vmem),
            scratch_shapes=scratch,
            compiler_params=pltpu.CompilerParams(
                collective_id=0, has_side_effects=True, vmem_limit_bytes=48 << 20
            ),
        )(inputs, out_grad, up_blocks, up_index, down_blocks, down_index)

    return jax.shard_map(
        body,
        mesh=mesh,
        in_specs=(
            P(("dp", "row"), "col"),
            P(("dp", "row"), "col"),
            P("row", "col", None, None, None),
            P("row", "col", None),
            P("row", "col", None, None, None),
            P("row", "col", None),
        ),
        out_specs=(
            P(("dp", "row"), "col"),
            P("row", "col", "dp", None, None),
            P("row", "col", "dp", None, None),
        ),
        check_vma=False,
    )
```

```python
import functools
import math

import jax
import jax.numpy as jnp
from jax import lax
from jax.experimental import pallas as pl
from jax.experimental.pallas import tpu as pltpu
from jax.sharding import PartitionSpec as P

MESH = pl.DeviceIdType.MESH
BF = jnp.bfloat16
F32 = jnp.float32
ROOT = math.sqrt(2.0 / math.pi)

BLK = 128
CAP = 16
KR = 12
NC = 6
HALF = 64
GATHER_TWOS = 3
PB = 3

DIRECT = (8, 4)


def tree(count, twos):
    strides = [2] * twos + [1] * (count - 2 * twos)
    marks = [0]
    for step in strides:
        marks.append(marks[-1] + step)
    return strides, marks


def gelu_parts(value):
    inner = ROOT * (value + 0.044715 * value * value * value)
    tanh_inner = jnp.tanh(inner)
    result = 0.5 * value * (1.0 + tanh_inner)
    slope = 0.5 * (1.0 + tanh_inner) + 0.5 * value * (
        1.0 - tanh_inner * tanh_inner
    ) * ROOT * (1.0 + 3.0 * 0.044715 * value * value)
    return result, slope


def nt_dot(a, b):
    return lax.dot_general(a, b, (((1,), (1,)), ((), ())), preferred_element_type=F32)


def kernel(
    sizes,
    x_hbm, g_hbm, wu_hbm, ui_ref, wd_hbm, di_ref,
    in_ref, up_ref, down_ref,
    xb, gb, wub, wdb, meta_v, meta_s, p_ref, a_ref, s_ref, pg_t, act_t,
    dw00, dw01, dw10, dw11, relay_in, relayed, one_in, half_sum, two_in,
    own, mine, theirs, ring_out, ring_leaf, ring_bone,
    first_l, meta_ss, meta_r, meta_l, wsend, whelp, wrecv, wlocal,
    ag_s, ag_r, sib_s, sib_r, sib_all,
    one_s, relay_r, one_r, two_s, two_r,
    part_s, part_r, ring_s, leaf_r, bone_r,
):
    nd, nr, nz = sizes
    tokens = BLK
    third = x_hbm.shape[0]
    width = third * HALF
    wide = 2 * third
    scale = 1.0 / math.sqrt(nd * nr * tokens)
    xg, wb = (xb, gb), (wub, wdb)
    dw = ((dw00, dw01), (dw10, dw11))
    d, r, c = lax.axis_index("dp"), lax.axis_index("row"), lax.axis_index("col")
    z, h = c // 2, c % 2
    sibling = (d, r, z * 2 + 1 - h)
    n_of = {1: nz // 2, -1: nz // 2 - 1}

    def xpeer(k):
        return (d, lax.rem(r + k, nr), c)

    def ypeer(k):
        return (lax.rem(d + k, nd), r, c)

    def zpeer(k):
        return (d, r, lax.rem(z + nz + k, nz) * 2 + h)

    def send(src, dst, ss, rs, to):
        copy = pltpu.make_async_remote_copy(
            src_ref=src, dst_ref=dst, send_sem=ss, recv_sem=rs, device_id=to, device_id_type=MESH
        )
        copy.start()

    def drain(ref, sem):
        pltpu.make_async_copy(ref, ref, sem).wait()

    own_rows = pl.ds(third * c, third)
    srcs = (x_hbm, g_hbm)
    firsts = [pltpu.make_async_copy(srcs[a], xg[a].at[own_rows], first_l.at[a]) for a in range(2)]
    srcw = (wu_hbm.at[0, 0], wd_hbm.at[0, 0])
    locals_ = [
        pltpu.make_async_copy(srcw[a], wb[a].at[pl.ds(CAP * r, CAP)], wlocal.at[a]) for a in range(2)
    ]
    for copy in firsts + locals_:
        copy.start()

    partners = [sibling] + [zpeer(k) for k in (1, -1, 2, -2)]
    partners += [xpeer(k) for k in range(1, nr)] + [ypeer(k) for k in range(1, nd)]
    barrier = pltpu.get_barrier_semaphore()
    for to in partners:
        pl.semaphore_signal(barrier, inc=1, device_id=to, device_id_type=MESH)

    pl.semaphore_wait(barrier, len(partners))

    def piece(a, k, core):
        where = lax.rem(z + nz + k, nz)
        return xg[a].at[pl.ds(wide * where + third * core, third)]

    def share(a, way, at):
        ref = piece(a, -way * at, h)
        arrived = sib_r.at[2 * at - 1 if way == 1 else 2 * at] if a == 0 else sib_all
        send(ref, ref, sib_s.at[a], arrived, sibling)

    trees = {way: tree(n_of[way], min(GATHER_TWOS, n_of[way] // 2)) for way in (1, -1)}

    def gather_send(a, way, at, hop):
        ref = piece(a, -way * at, h)
        side = 0 if way == 1 else 1
        send(ref, ref, ag_s.at[a], ag_r.at[a, side, at + hop - 1], zpeer(way * hop))

    def gather_wait(a, way, at):
        side = 0 if way == 1 else 1
        drain(piece(a, -way * at, h), ag_r.at[a, side, at - 1])

    def gather_step(a, way, j):
        strides, marks = trees[way]
        if j > len(strides):
            return
        at = marks[j]
        if j > 0:
            gather_wait(a, way, at)
        if j < len(strides):
            gather_send(a, way, at, strides[j])
            if strides[j] == 2:
                gather_send(a, way, at, 1)
        if j > 0:
            share(a, way, at)

    def gather_leaf(a, way, j):
        strides, marks = trees[way]
        if 0 < j <= len(strides) and strides[j - 1] == 2:
            gather_wait(a, way, marks[j] - 1)
            share(a, way, marks[j] - 1)

    for a in range(2):
        firsts[a].wait()
        for way in (1, -1):
            gather_step(a, way, 0)
    for a in range(2):
        share(a, -1, 0)

    per = [(CAP - direct) // nd for direct in DIRECT]

    def weights_help(a):
        for k in range(1, nr):
            send(
                srcw[a].at[pl.ds(per[a] * d, per[a])], wb[a].at[pl.ds(CAP * r + per[a] * d, per[a])],
                wsend.at[a], whelp.at[a, k], xpeer(k),
            )

    def weights_direct(a):
        for k in range(1, nr):
            send(
                srcw[a].at[pl.ds(CAP - DIRECT[a], DIRECT[a])],
                wb[a].at[pl.ds(CAP * r + CAP - DIRECT[a], DIRECT[a])],
                wsend.at[a], wrecv.at[a], xpeer(k),
            )

    weights_help(0)
    weights_help(1)
    weights_direct(0)

    lane = lax.broadcasted_iota(jnp.int32, (8, BLK), 1)
    line = lax.broadcasted_iota(jnp.int32, (8, BLK), 0)

    def publish():
        table = jnp.where(line >= 6, nr * CAP, 0)
        for s in range(CAP):
            up = ui_ref[0, 0, s]
            down = di_ref[0, 0, s]
            up_ok, down_ok = up >= 0, down >= 0
            up_p, down_p = jnp.maximum(up, 0), jnp.maximum(down, 0)
            entries = (
                r * KR + up_p // NC, up_p % NC, up_ok.astype(jnp.int32),
                down_p // KR, r * KR + down_p % KR, down_ok.astype(jnp.int32),
            )
            for i, entry in enumerate(entries):
                table = jnp.where((line == i) & (lane == s), entry, table)
            table = jnp.where((line == 6) & (lane == up), r * CAP + s, table)
            table = jnp.where((line == 7) & (lane == down), r * CAP + s, table)
        meta_v[r] = table
        for k in range(1, nr):
            send(meta_v.at[r], meta_v.at[r], meta_ss.at[k], meta_r.at[k], xpeer(k))
        for a in range(2):
            wb[a][nr * CAP] = jnp.zeros((BLK, BLK), BF)

    def help_on(a):
        for k in range(1, nr):
            src = lax.rem(r + nr - k, nr)
            ref = wb[a].at[pl.ds(CAP * src + per[a] * d, per[a])]
            drain(ref, whelp.at[a, k])
            for ky in range(1, nd):
                send(ref, ref, wsend.at[a], wrecv.at[a], ypeer(ky))

    sum_trees = {way: tree(n_of[way], n_of[way] // 2) for way in (1, -1)}

    weights_direct(1)
    publish()
    p_ref[...] = jnp.zeros_like(p_ref)
    a_ref[...] = jnp.zeros_like(a_ref)

    def tables():
        for k in range(1, nr):
            src = lax.rem(r + nr - k, nr)
            drain(meta_v.at[src], meta_r.at[k])
        to_smem = pltpu.make_async_copy(meta_v, meta_s, meta_l)
        to_smem.start()
        to_smem.wait()

    def weights_here(a):
        locals_[a].wait()
        got = (nr - 1) * DIRECT[a] + (nr - 1) * (nd - 1) * per[a]
        drain(wb[a].at[pl.ds(0, got)], wrecv.at[a])

    def forward(low, high):
        @pl.loop(low, high)
        def _(i):
            at = (i + 1) // 2
            where = lax.rem(z + nz + at * (1 - 2 * (i % 2)), nz)
            drain(xb.at[pl.ds(wide * where + third * (1 - h), third)], sib_r.at[i])
            owner = where // (KR // PB)
            base = (where % (KR // PB)) * PB
            left = xb[pl.ds(wide * where, wide)].reshape(wide * HALF, tokens).T
            right = jnp.concatenate(
                [
                    jnp.concatenate(
                        [wub[meta_s[owner, 6, (base + i) * NC + j]] for j in range(NC)], axis=1
                    )
                    for i in range(PB)
                ],
                axis=0,
            )
            p_ref[...] += jnp.dot(left, right, preferred_element_type=F32)

    longest = max(len(trees[way][0]) for way in (1, -1))
    for j in range(1, longest + 1):
        for a in range(2):
            for way in (1, -1):
                gather_step(a, way, j)
        for a in range(2):
            for way in (1, -1):
                gather_leaf(a, way, j)
        if j <= 2:
            help_on(j - 1)
    tables()
    weights_here(0)
    forward(0, nz)
    drain(xg[1].at[pl.ds(0, third * nz)], sib_all)

    step_rows = 4
    steps = nr * KR // step_rows
    per_owner = KR // step_rows
    deep = step_rows * BLK

    act, slope = gelu_parts(p_ref[...])
    act_low = act.astype(BF)
    for i in range(NC):
        act_t[i] = act_low[:, i * BLK:(i + 1) * BLK].T
        s_ref[pl.ds(i * BLK, BLK), :] = slope[:, i * BLK:(i + 1) * BLK].T

    def block_rows(ref, k):
        return jnp.concatenate([ref[2 * k], ref[2 * k + 1]], axis=0)

    ways = ((r, nr, xpeer), (d, nd, ypeer))
    share_y = CAP // nd
    part = share_y // 2

    def terms(a, e, k):
        place, count, _ = ways[e]
        first = lax.rem(place + k, count)

        @pl.loop(0, ways[1 - e][1])
        def _(second):
            owner, owner_y = (first, second) if e == 0 else (second, first)
            for u in range(part):
                s = share_y * owner_y + part * e + u
                if a == 0:
                    i, j = meta_s[owner, 3, s], meta_s[owner, 4, s]
                    keep = meta_s[owner, 5, s].astype(F32) * scale
                    term = nt_dot(act_t[i], block_rows(gb, j))
                else:
                    i, j = meta_s[owner, 0, s], meta_s[owner, 1, s]
                    keep = meta_s[owner, 2, s].astype(F32) * scale
                    term = nt_dot(block_rows(xb, i), pg_t[j])
                dw[a][e][k, second, u] = (term * keep).astype(BF)

    def halves(a, e, k, side):
        return dw[a][e].at[k, pl.ds(2 * side, 2)]

    def relay_out(a, e):
        for side, k in ((0, 1), (1, 3)):
            send(halves(a, e, 2, side), relay_in.at[a, e, side], one_s.at[a, e], relay_r.at[a, e, side], ways[e][2](k))

    def direct_out(a, e, k):
        side = 1 if k == 1 else 0
        send(halves(a, e, k, side), one_in.at[a, e, k // 2, side], one_s.at[a, e], one_r.at[a, e, k // 2, side], ways[e][2](k))

    def relay_on(a, e):
        for side, k in ((0, 1), (1, 3)):
            drain(relay_in.at[a, e, side], relay_r.at[a, e, side])

            @pl.loop(0, 2)
            def _(t):
                for u in range(part):
                    total = dw[a][e][k, 2 * side + t, u].astype(F32) + relay_in[a, e, side, t, u].astype(F32)
                    relayed[a, e, side, t, u] = total.astype(BF)

            send(
                relayed.at[a, e, side], one_in.at[a, e, k // 2, side], one_s.at[a, e],
                one_r.at[a, e, k // 2, side], ways[e][2](k),
            )

    def second_out(a, e):
        for k in range(2):
            for side in range(2):
                drain(one_in.at[a, e, k, side], one_r.at[a, e, k, side])

        @pl.loop(0, 2)
        def _(t):
            for side in range(2):
                for u in range(part):
                    total = dw[a][e][0, 2 * side + t, u].astype(F32)
                    for k in range(2):
                        total += one_in[a, e, k, side, t, u].astype(F32)
                    half_sum[a, e, 2 * side + t, u] = total.astype(BF)

        place, count, peer = ways[1 - e]
        for k in (2, 1, 3):
            to = lax.rem(place + k, count)
            send(half_sum.at[a, e, to], two_in.at[a, e, k - 1], two_s.at[a, e], two_r.at[a, e, k - 1], peer(k))

    def finish(a, e):
        place, count, _ = ways[1 - e]
        for k in range(count - 1):
            drain(two_in.at[a, e, k], two_r.at[a, e, k])
        out = (down_ref, up_ref)[a]
        for u in range(part):
            total = half_sum[a, e, place, u].astype(F32)
            for k in range(count - 1):
                total += two_in[a, e, k, u].astype(F32)
            out[0, 0, part * e + u] = total.astype(BF)

    def act_gradient():
        weights_here(1)

        @pl.loop(0, steps)
        def _(t):
            owner, base = t // per_owner, (t % per_owner) * step_rows
            right = gb[pl.ds(2 * step_rows * t, 2 * step_rows)].reshape(deep, tokens)
            left = jnp.concatenate(
                [
                    jnp.concatenate(
                        [wdb[meta_s[owner, 7, i * KR + base + j]] for j in range(step_rows)], axis=1
                    )
                    for i in range(NC)
                ],
                axis=0,
            )
            a_ref[...] += jnp.dot(left, right, preferred_element_type=F32)

        for i in range(NC):
            rows = pl.ds(i * BLK, BLK)
            pg_t[i] = (a_ref[rows, :] * s_ref[rows, :]).astype(BF)

    def partial_piece(index, k):
        where = lax.rem(z + nz + k, nz)
        owner = where // (KR // PB)
        base = (where % (KR // PB)) * PB
        left = jnp.concatenate(
            [
                jnp.concatenate(
                    [wub[meta_s[owner, 6, (base + i) * NC + j]] for j in range(NC)], axis=1
                )
                for i in range(PB)
            ],
            axis=0,
        )
        right = jnp.concatenate([pg_t[j] for j in range(NC)], axis=0)
        own[index] = jnp.dot(left, right, preferred_element_type=F32).reshape(2, width, tokens)
        mine[index] = own[index, 1 - h].astype(BF)
        send(mine.at[index], theirs.at[index], part_s, part_r.at[index], sibling)

    n_right, n_left = n_of[1], n_of[-1]

    def index_of(way, at):
        return at - 1 if way == 1 else n_right + at - 1

    order = []
    for at in range(n_right, 0, -1):
        order.append((1, at))
        if at <= n_left:
            order.append((-1, at))
    def summed(index, extra):
        drain(theirs.at[index], part_r.at[index])
        total = own[index, h] + theirs[index].astype(F32)
        for ref in extra:
            total = total + ref[...].astype(F32)
        return total

    def incoming(way, at):
        strides, marks = sum_trees[way]
        side = 0 if way == 1 else 1
        refs = []
        j = marks.index(at)
        if j < len(strides):
            if strides[j] == 2:
                refs.append((ring_leaf.at[side, at], leaf_r.at[side, at]))
            refs.append((ring_bone.at[side, at], bone_r.at[side, at]))
        return refs

    def ring_step(way, at):
        strides, marks = sum_trees[way]
        side = 0 if way == 1 else 1
        index = index_of(way, at)
        ref = ring_out.at[index]
        if at in marks:
            pairs = incoming(way, at)
            for more, sem in pairs:
                drain(more, sem)
            hop = strides[marks.index(at) - 1]
            ref[...] = summed(index, [more for more, _ in pairs]).astype(BF)
            send(ref, ring_bone.at[side, at - hop], ring_s, bone_r.at[side, at - hop], zpeer(way * hop))
        else:
            ref[...] = summed(index, []).astype(BF)
            send(ref, ring_leaf.at[side, at - 1], ring_s, leaf_r.at[side, at - 1], zpeer(way))

    def waits(way, at):
        return at in sum_trees[way][1][:-1]

    def ring_chain(level):
        for way in (1, -1):
            inner = sum_trees[way][1][1:-1][::-1]
            if level < len(inner):
                ring_step(way, inner[level])

    def ring_end():
        pairs = incoming(1, 0) + incoming(-1, 0)
        for ref, sem in pairs:
            drain(ref, sem)
        in_ref[...] = summed(nz - 1, [ref for ref, _ in pairs]).astype(BF)

    for e in (0, 1):
        terms(0, e, 2)
        relay_out(0, e)
    act_gradient()
    for e in (0, 1):
        terms(1, e, 2)
        relay_out(1, e)
    last = None
    for way, at in order:
        partial_piece(index_of(way, at), way * at)
        if last is not None and not waits(*last):
            ring_step(*last)
        last = (way, at)
    if not waits(*last):
        ring_step(*last)
    for a in (0, 1):
        for e in (0, 1):
            for k in (1, 3):
                terms(a, e, k)
                direct_out(a, e, k)
        if a == 0:
            ring_chain(0)
            for e in (0, 1):
                relay_on(a, e)
    ring_chain(1)
    partial_piece(nz - 1, 0)
    for e in (0, 1):
        relay_on(1, e)
    for a in (0, 1):
        for e in (0, 1):
            terms(a, e, 0)
    ring_chain(2)
    for e in (0, 1):
        second_out(0, e)
    ring_end()
    for e in (0, 1):
        second_out(1, e)
    for a in (0, 1):
        for e in (0, 1):
            finish(a, e)

    for a in range(2):
        drain(xg[a].at[pl.ds(0, third * (nz - 1))], ag_s.at[a])
        drain(xg[a].at[pl.ds(0, third * nz)], sib_s.at[a])
        gone = (nr - 1) * (per[a] + DIRECT[a]) + (nr - 1) * (nd - 1) * per[a]
        drain(wb[a].at[pl.ds(0, gone)], wsend.at[a])
    for k in range(1, nr):
        drain(meta_v.at[r], meta_ss.at[k])
    for a in range(2):
        for e in range(2):
            for _ in range(3):
                drain(relay_in.at[a, e], one_s.at[a, e])
            drain(two_in.at[a, e], two_s.at[a, e])

    drain(mine, part_s)
    drain(ring_out, ring_s)


def solution(mesh):
    nd, nr, nc = mesh.shape["dp"], mesh.shape["row"], mesh.shape["col"]
    nz = nc // 2
    DMA = pltpu.SemaphoreType.DMA
    VMEM = pltpu.VMEM

    def body(inputs, out_grad, up_blocks, up_index, down_blocks, down_index):
        tokens, width = inputs.shape
        blocks = nr * KR
        hidden = NC * BLK
        share = CAP // nd
        vmem = pl.BlockSpec(memory_space=pltpu.VMEM)
        smem = pl.BlockSpec(memory_space=pltpu.SMEM)
        hbm = pl.BlockSpec(memory_space=pltpu.HBM)
        scratch = [
            VMEM((blocks * BLK // HALF, HALF, tokens), BF),
            VMEM((blocks * BLK // HALF, HALF, tokens), BF),
            VMEM((nr * CAP + 1, BLK, BLK), BF),
            VMEM((nr * CAP + 1, BLK, BLK), BF),
            VMEM((nr, 8, BLK), jnp.int32),
            pltpu.SMEM((nr, 8, BLK), jnp.int32),
            VMEM((tokens, hidden), F32),
            VMEM((hidden, tokens), F32),
            VMEM((hidden, tokens), F32),
            VMEM((NC, BLK, tokens), BF),
            VMEM((NC, BLK, tokens), BF),
            VMEM((nr, nd, share // 2, BLK, BLK), BF),
            VMEM((nd, nr, share // 2, BLK, BLK), BF),
            VMEM((nr, nd, share // 2, BLK, BLK), BF),
            VMEM((nd, nr, share // 2, BLK, BLK), BF),
            VMEM((2, 2, 2, 2, share // 2, BLK, BLK), BF),
            VMEM((2, 2, 2, 2, share // 2, BLK, BLK), BF),
            VMEM((2, 2, 2, 2, 2, share // 2, BLK, BLK), BF),
            VMEM((2, 2, 4, share // 2, BLK, BLK), BF),
            VMEM((2, 2, 3, share // 2, BLK, BLK), BF),
            VMEM((nz, 2, width, tokens), F32),
            VMEM((nz, width, tokens), BF),
            VMEM((nz, width, tokens), BF),
            VMEM((nz - 1, width, tokens), BF),
            VMEM((2, nz // 2, width, tokens), BF),
            VMEM((2, nz // 2, width, tokens), BF),
            DMA((2,)),
            DMA((nr,)), DMA((nr,)), DMA,
            DMA((2,)), DMA((2, nr)), DMA((2,)), DMA((2,)),
            DMA((2,)), DMA((2, 2, nz // 2)),
            DMA((2,)), DMA((nz,)), DMA,
            DMA((2, 2)), DMA((2, 2, 2)), DMA((2, 2, 2, 2)),
            DMA((2, 2)), DMA((2, 2, 3)),
            DMA, DMA((nz,)),
            DMA, DMA((2, nz // 2)), DMA((2, nz // 2)),
        ]
        def units(array):
            return array.T.reshape(width // HALF, HALF, tokens)

        in_grad, up_grad, down_grad = pl.pallas_call(
            functools.partial(kernel, (nd, nr, nz)),
            out_shape=(
                jax.ShapeDtypeStruct((width, tokens), BF),
                jax.ShapeDtypeStruct((1, 1, share, BLK, BLK), BF),
                jax.ShapeDtypeStruct((1, 1, share, BLK, BLK), BF),
            ),
            in_specs=[hbm, hbm, hbm, smem, hbm, smem],
            out_specs=(vmem, vmem, vmem),
            scratch_shapes=scratch,
            compiler_params=pltpu.CompilerParams(
                collective_id=0, has_side_effects=True, vmem_limit_bytes=60 << 20
            ),
        )(units(inputs), units(out_grad), up_blocks, up_index, down_blocks, down_index)
        return in_grad.T, up_grad, down_grad

    return jax.shard_map(
        body,
        mesh=mesh,
        in_specs=(
            P(("dp", "row"), "col"),
            P(("dp", "row"), "col"),
            P("row", "col", None, None, None),
            P("row", "col", None),
            P("row", "col", None, None, None),
            P("row", "col", None),
        ),
        out_specs=(
            P(("dp", "row"), "col"),
            P("row", "col", "dp", None, None),
            P("row", "col", "dp", None, None),
        ),
        check_vma=False,
    )
```

```python
import functools
import math

import jax
import jax.numpy as jnp
from jax import lax
from jax.experimental import pallas as pl
from jax.experimental.pallas import tpu as pltpu
from jax.sharding import PartitionSpec as P

MESH = pl.DeviceIdType.MESH
BF = jnp.bfloat16
F32 = jnp.float32
ROOT = math.sqrt(2.0 / math.pi)

BLK = 128
CAP = 16
KR = 12
NC = 6
HALF = 64
GATHER_TWOS = 3
PB = 3

DIRECT = (8, 4)


def tree(count, twos):
    strides = [2] * twos + [1] * (count - 2 * twos)
    marks = [0]
    for step in strides:
        marks.append(marks[-1] + step)
    return strides, marks


def gelu_parts(value):
    inner = ROOT * (value + 0.044715 * value * value * value)
    tanh_inner = jnp.tanh(inner)
    result = 0.5 * value * (1.0 + tanh_inner)
    slope = 0.5 * (1.0 + tanh_inner) + 0.5 * value * (
        1.0 - tanh_inner * tanh_inner
    ) * ROOT * (1.0 + 3.0 * 0.044715 * value * value)
    return result, slope


def nt_dot(a, b):
    return lax.dot_general(a, b, (((1,), (1,)), ((), ())), preferred_element_type=F32)


def kernel(
    sizes,
    x_hbm, g_hbm, wu_hbm, ui_ref, wd_hbm, di_ref,
    in_ref, up_ref, down_ref,
    xb, gb, wub, wdb, meta_v, meta_s, p_ref, a_ref, s_ref, pg_t, act_t,
    dw00, dw01, dw10, dw11, relay_in, relayed, one_in, half_sum, two_in,
    own, mine, theirs, ring_out, ring_leaf, ring_bone,
    first_l, meta_ss, meta_r, meta_l, wsend, whelp, wrecv, wlocal,
    ag_s, ag_r, sib_s, sib_r, sib_all,
    one_s, relay_r, one_r, two_s, two_r,
    part_s, part_r, ring_s, leaf_r, bone_r,
):
    nd, nr, nz = sizes
    tokens = BLK
    third = x_hbm.shape[0]
    width = third * HALF
    wide = 2 * third
    scale = 1.0 / math.sqrt(nd * nr * tokens)
    xg, wb = (xb, gb), (wub, wdb)
    dw = ((dw00, dw01), (dw10, dw11))
    d, r, c = lax.axis_index("dp"), lax.axis_index("row"), lax.axis_index("col")
    z, h = c // 2, c % 2
    sibling = (d, r, z * 2 + 1 - h)
    n_of = {1: nz // 2, -1: nz // 2 - 1}

    def xpeer(k):
        return (d, lax.rem(r + k, nr), c)

    def ypeer(k):
        return (lax.rem(d + k, nd), r, c)

    def zpeer(k):
        return (d, r, lax.rem(z + nz + k, nz) * 2 + h)

    def send(src, dst, ss, rs, to):
        copy = pltpu.make_async_remote_copy(
            src_ref=src, dst_ref=dst, send_sem=ss, recv_sem=rs, device_id=to, device_id_type=MESH
        )
        copy.start()

    def drain(ref, sem):
        pltpu.make_async_copy(ref, ref, sem).wait()

    own_rows = pl.ds(third * c, third)
    srcs = (x_hbm, g_hbm)
    firsts = [pltpu.make_async_copy(srcs[a], xg[a].at[own_rows], first_l.at[a]) for a in range(2)]
    srcw = (wu_hbm.at[0, 0], wd_hbm.at[0, 0])
    locals_ = [
        pltpu.make_async_copy(srcw[a], wb[a].at[pl.ds(CAP * r, CAP)], wlocal.at[a]) for a in range(2)
    ]
    for copy in firsts + locals_:
        copy.start()

    partners = [sibling] + [zpeer(k) for k in (1, -1, 2, -2)]
    partners += [xpeer(k) for k in range(1, nr)] + [ypeer(k) for k in range(1, nd)]
    barrier = pltpu.get_barrier_semaphore()
    for to in partners:
        pl.semaphore_signal(barrier, inc=1, device_id=to, device_id_type=MESH)

    pl.semaphore_wait(barrier, len(partners))

    def piece(a, k, core):
        where = lax.rem(z + nz + k, nz)
        return xg[a].at[pl.ds(wide * where + third * core, third)]

    def share(a, way, at):
        ref = piece(a, -way * at, h)
        arrived = sib_r.at[2 * at - 1 if way == 1 else 2 * at] if a == 0 else sib_all
        send(ref, ref, sib_s.at[a], arrived, sibling)

    trees = {way: tree(n_of[way], min(GATHER_TWOS, n_of[way] // 2)) for way in (1, -1)}

    def gather_send(a, way, at, hop):
        ref = piece(a, -way * at, h)
        side = 0 if way == 1 else 1
        send(ref, ref, ag_s.at[a], ag_r.at[a, side, at + hop - 1], zpeer(way * hop))

    def gather_wait(a, way, at):
        side = 0 if way == 1 else 1
        drain(piece(a, -way * at, h), ag_r.at[a, side, at - 1])

    def gather_step(a, way, j):
        strides, marks = trees[way]
        if j > len(strides):
            return
        at = marks[j]
        if j > 0:
            gather_wait(a, way, at)
        if j < len(strides):
            gather_send(a, way, at, strides[j])
            if strides[j] == 2:
                gather_send(a, way, at, 1)
        if j > 0:
            share(a, way, at)

    def gather_leaf(a, way, j):
        strides, marks = trees[way]
        if 0 < j <= len(strides) and strides[j - 1] == 2:
            gather_wait(a, way, marks[j] - 1)
            share(a, way, marks[j] - 1)

    for a in range(2):
        firsts[a].wait()
        for way in (1, -1):
            gather_step(a, way, 0)
    for a in range(2):
        share(a, -1, 0)

    per = [(CAP - direct) // nd for direct in DIRECT]

    def weights_help(a):
        for k in range(1, nr):
            send(
                srcw[a].at[pl.ds(per[a] * d, per[a])], wb[a].at[pl.ds(CAP * r + per[a] * d, per[a])],
                wsend.at[a], whelp.at[a, k], xpeer(k),
            )

    def weights_direct(a):
        for k in range(1, nr):
            send(
                srcw[a].at[pl.ds(CAP - DIRECT[a], DIRECT[a])],
                wb[a].at[pl.ds(CAP * r + CAP - DIRECT[a], DIRECT[a])],
                wsend.at[a], wrecv.at[a], xpeer(k),
            )

    weights_help(0)
    weights_help(1)
    weights_direct(0)

    lane = lax.broadcasted_iota(jnp.int32, (8, BLK), 1)
    line = lax.broadcasted_iota(jnp.int32, (8, BLK), 0)

    def publish():
        table = jnp.where(line >= 6, nr * CAP, 0)
        for s in range(CAP):
            up = ui_ref[0, 0, s]
            down = di_ref[0, 0, s]
            up_ok, down_ok = up >= 0, down >= 0
            up_p, down_p = jnp.maximum(up, 0), jnp.maximum(down, 0)
            entries = (
                r * KR + up_p // NC, up_p % NC, up_ok.astype(jnp.int32),
                down_p // KR, r * KR + down_p % KR, down_ok.astype(jnp.int32),
            )
            for i, entry in enumerate(entries):
                table = jnp.where((line == i) & (lane == s), entry, table)
            table = jnp.where((line == 6) & (lane == up), r * CAP + s, table)
            table = jnp.where((line == 7) & (lane == down), r * CAP + s, table)
        meta_v[r] = table
        for k in range(1, nr):
            send(meta_v.at[r], meta_v.at[r], meta_ss.at[k], meta_r.at[k], xpeer(k))
        for a in range(2):
            wb[a][nr * CAP] = jnp.zeros((BLK, BLK), BF)

    def help_on(a):
        for k in range(1, nr):
            src = lax.rem(r + nr - k, nr)
            ref = wb[a].at[pl.ds(CAP * src + per[a] * d, per[a])]
            drain(ref, whelp.at[a, k])
            for ky in range(1, nd):
                send(ref, ref, wsend.at[a], wrecv.at[a], ypeer(ky))

    sum_trees = {way: tree(n_of[way], n_of[way] // 2) for way in (1, -1)}

    weights_direct(1)
    publish()
    p_ref[...] = jnp.zeros_like(p_ref)
    a_ref[...] = jnp.zeros_like(a_ref)

    def tables():
        for k in range(1, nr):
            src = lax.rem(r + nr - k, nr)
            drain(meta_v.at[src], meta_r.at[k])
        to_smem = pltpu.make_async_copy(meta_v, meta_s, meta_l)
        to_smem.start()
        to_smem.wait()

    def weights_here(a):
        locals_[a].wait()
        got = (nr - 1) * DIRECT[a] + (nr - 1) * (nd - 1) * per[a]
        drain(wb[a].at[pl.ds(0, got)], wrecv.at[a])

    def forward():
        for i in range(nz):
            at = (i + 1) // 2
            where = lax.rem(z + nz + at * (1 - 2 * (i % 2)), nz)
            drain(xb.at[pl.ds(wide * where + third * (1 - h), third)], sib_r.at[i])

        @pl.loop(0, nr)
        def _(owner):
            deep = KR * BLK
            left = xb[pl.ds(2 * KR * owner, 2 * KR)].reshape(deep, tokens).T
            right = jnp.concatenate(
                [
                    jnp.concatenate([wub[meta_s[owner, 6, i * NC + j]] for j in range(NC)], axis=1)
                    for i in range(KR)
                ],
                axis=0,
            )
            p_ref[...] += jnp.dot(left, right, preferred_element_type=F32)

    longest = max(len(trees[way][0]) for way in (1, -1))
    for j in range(1, longest + 1):
        for a in range(2):
            for way in (1, -1):
                gather_step(a, way, j)
        for a in range(2):
            for way in (1, -1):
                gather_leaf(a, way, j)
        if j <= 2:
            help_on(j - 1)
    tables()
    weights_here(0)
    forward()
    drain(xg[1].at[pl.ds(0, third * nz)], sib_all)

    step_rows = 12
    steps = nr * KR // step_rows
    per_owner = KR // step_rows
    deep = step_rows * BLK

    act, slope = gelu_parts(p_ref[...])
    act_low = act.astype(BF)
    for i in range(NC):
        act_t[i] = act_low[:, i * BLK:(i + 1) * BLK].T
        s_ref[pl.ds(i * BLK, BLK), :] = slope[:, i * BLK:(i + 1) * BLK].T

    def block_rows(ref, k):
        return jnp.concatenate([ref[2 * k], ref[2 * k + 1]], axis=0)

    ways = ((r, nr, xpeer), (d, nd, ypeer))
    share_y = CAP // nd
    part = share_y // 2

    def terms(a, e, k):
        place, count, _ = ways[e]
        first = lax.rem(place + k, count)

        @pl.loop(0, ways[1 - e][1], unroll=2)
        def _(second):
            owner, owner_y = (first, second) if e == 0 else (second, first)
            for u in range(part):
                s = share_y * owner_y + part * e + u
                if a == 0:
                    i, j = meta_s[owner, 3, s], meta_s[owner, 4, s]
                    keep = meta_s[owner, 5, s].astype(F32) * scale
                    term = nt_dot(act_t[i], block_rows(gb, j))
                else:
                    i, j = meta_s[owner, 0, s], meta_s[owner, 1, s]
                    keep = meta_s[owner, 2, s].astype(F32) * scale
                    term = nt_dot(block_rows(xb, i), pg_t[j])
                dw[a][e][k, second, u] = (term * keep).astype(BF)

    def halves(a, e, k, side):
        return dw[a][e].at[k, pl.ds(2 * side, 2)]

    def relay_out(a, e):
        for side, k in ((0, 1), (1, 3)):
            send(halves(a, e, 2, side), relay_in.at[a, e, side], one_s.at[a, e], relay_r.at[a, e, side], ways[e][2](k))

    def direct_out(a, e, k):
        side = 1 if k == 1 else 0
        send(halves(a, e, k, side), one_in.at[a, e, k // 2, side], one_s.at[a, e], one_r.at[a, e, k // 2, side], ways[e][2](k))

    def relay_on(a, e):
        for side, k in ((0, 1), (1, 3)):
            drain(relay_in.at[a, e, side], relay_r.at[a, e, side])

            @pl.loop(0, 2)
            def _(t):
                for u in range(part):
                    total = dw[a][e][k, 2 * side + t, u].astype(F32) + relay_in[a, e, side, t, u].astype(F32)
                    relayed[a, e, side, t, u] = total.astype(BF)

            send(
                relayed.at[a, e, side], one_in.at[a, e, k // 2, side], one_s.at[a, e],
                one_r.at[a, e, k // 2, side], ways[e][2](k),
            )

    def second_out(a, e):
        for k in range(2):
            for side in range(2):
                drain(one_in.at[a, e, k, side], one_r.at[a, e, k, side])

        @pl.loop(0, 2)
        def _(t):
            for side in range(2):
                for u in range(part):
                    total = dw[a][e][0, 2 * side + t, u].astype(F32)
                    for k in range(2):
                        total += one_in[a, e, k, side, t, u].astype(F32)
                    half_sum[a, e, 2 * side + t, u] = total.astype(BF)

        place, count, peer = ways[1 - e]
        for k in (2, 1, 3):
            to = lax.rem(place + k, count)
            send(half_sum.at[a, e, to], two_in.at[a, e, k - 1], two_s.at[a, e], two_r.at[a, e, k - 1], peer(k))

    def finish(a, e):
        place, count, _ = ways[1 - e]
        for k in range(count - 1):
            drain(two_in.at[a, e, k], two_r.at[a, e, k])
        out = (down_ref, up_ref)[a]
        for u in range(part):
            total = half_sum[a, e, place, u].astype(F32)
            for k in range(count - 1):
                total += two_in[a, e, k, u].astype(F32)
            out[0, 0, part * e + u] = total.astype(BF)

    def act_gradient():
        weights_here(1)

        @pl.loop(0, steps)
        def _(t):
            owner, base = t // per_owner, (t % per_owner) * step_rows
            right = gb[pl.ds(2 * step_rows * t, 2 * step_rows)].reshape(deep, tokens)
            left = jnp.concatenate(
                [
                    jnp.concatenate(
                        [wdb[meta_s[owner, 7, i * KR + base + j]] for j in range(step_rows)], axis=1
                    )
                    for i in range(NC)
                ],
                axis=0,
            )
            a_ref[...] += jnp.dot(left, right, preferred_element_type=F32)

        for i in range(NC):
            rows = pl.ds(i * BLK, BLK)
            pg_t[i] = (a_ref[rows, :] * s_ref[rows, :]).astype(BF)

    def partial_piece(index, k):
        partial_store(index, partial_dot(k))

    def partial_dot(k):
        where = lax.rem(z + nz + k, nz)
        owner = where // (KR // PB)
        base = (where % (KR // PB)) * PB
        left = jnp.concatenate(
            [
                jnp.concatenate(
                    [wub[meta_s[owner, 6, (base + i) * NC + j]] for j in range(NC)], axis=1
                )
                for i in range(PB)
            ],
            axis=0,
        )
        right = jnp.concatenate([pg_t[j] for j in range(NC)], axis=0)
        return jnp.dot(left, right, preferred_element_type=F32)

    def partial_store(index, both):
        own[index] = both.reshape(2, width, tokens)
        mine[index] = own[index, 1 - h].astype(BF)
        send(mine.at[index], theirs.at[index], part_s, part_r.at[index], sibling)

    n_right, n_left = n_of[1], n_of[-1]

    def index_of(way, at):
        return at - 1 if way == 1 else n_right + at - 1

    order = []
    for at in range(n_right, 0, -1):
        order.append((1, at))
        if at <= n_left:
            order.append((-1, at))
    def summed(index, extra):
        drain(theirs.at[index], part_r.at[index])
        total = own[index, h] + theirs[index].astype(F32)
        for ref in extra:
            total = total + ref[...].astype(F32)
        return total

    def incoming(way, at):
        strides, marks = sum_trees[way]
        side = 0 if way == 1 else 1
        refs = []
        j = marks.index(at)
        if j < len(strides):
            if strides[j] == 2:
                refs.append((ring_leaf.at[side, at], leaf_r.at[side, at]))
            refs.append((ring_bone.at[side, at], bone_r.at[side, at]))
        return refs

    def ring_step(way, at):
        strides, marks = sum_trees[way]
        side = 0 if way == 1 else 1
        index = index_of(way, at)
        ref = ring_out.at[index]
        if at in marks:
            pairs = incoming(way, at)
            for more, sem in pairs:
                drain(more, sem)
            hop = strides[marks.index(at) - 1]
            ref[...] = summed(index, [more for more, _ in pairs]).astype(BF)
            send(ref, ring_bone.at[side, at - hop], ring_s, bone_r.at[side, at - hop], zpeer(way * hop))
        else:
            ref[...] = summed(index, []).astype(BF)
            send(ref, ring_leaf.at[side, at - 1], ring_s, leaf_r.at[side, at - 1], zpeer(way))

    def waits(way, at):
        return at in sum_trees[way][1][:-1]

    def ring_chain(level):
        for way in (1, -1):
            inner = sum_trees[way][1][1:-1][::-1]
            if level < len(inner):
                ring_step(way, inner[level])

    def ring_end():
        pairs = incoming(1, 0) + incoming(-1, 0)
        for ref, sem in pairs:
            drain(ref, sem)
        in_ref[...] = summed(nz - 1, [ref for ref, _ in pairs]).astype(BF)

    for e in (0, 1):
        terms(0, e, 2)
        relay_out(0, e)
    act_gradient()
    for e in (0, 1):
        terms(1, e, 2)
        relay_out(1, e)
    before = []
    for at in range(n_right, 0, -1):
        both = [(way, at) for way in (1, -1) if at <= n_of[way]]
        dots = [partial_dot(way * at) for way, at in both]
        for (way, at), value in zip(both, dots):
            partial_store(index_of(way, at), value)
        for one in before:
            if not waits(*one):
                ring_step(*one)
        before = both
    for one in before:
        if not waits(*one):
            ring_step(*one)
    for a in (0, 1):
        for e in (0, 1):
            for k in (1, 3):
                terms(a, e, k)
                direct_out(a, e, k)
        if a == 0:
            ring_chain(0)
            for e in (0, 1):
                relay_on(a, e)
    ring_chain(1)
    partial_piece(nz - 1, 0)
    for e in (0, 1):
        relay_on(1, e)
    for a in (0, 1):
        for e in (0, 1):
            terms(a, e, 0)
    ring_chain(2)
    for e in (0, 1):
        second_out(0, e)
    ring_end()
    for e in (0, 1):
        second_out(1, e)
    for a in (0, 1):
        for e in (0, 1):
            finish(a, e)

    for a in range(2):
        drain(xg[a].at[pl.ds(0, third * (nz - 1))], ag_s.at[a])
        drain(xg[a].at[pl.ds(0, third * nz)], sib_s.at[a])
        gone = (nr - 1) * (per[a] + DIRECT[a]) + (nr - 1) * (nd - 1) * per[a]
        drain(wb[a].at[pl.ds(0, gone)], wsend.at[a])
    for k in range(1, nr):
        drain(meta_v.at[r], meta_ss.at[k])
    for a in range(2):
        for e in range(2):
            for _ in range(3):
                drain(relay_in.at[a, e], one_s.at[a, e])
            drain(two_in.at[a, e], two_s.at[a, e])

    drain(mine, part_s)
    drain(ring_out, ring_s)


def solution(mesh):
    nd, nr, nc = mesh.shape["dp"], mesh.shape["row"], mesh.shape["col"]
    nz = nc // 2
    DMA = pltpu.SemaphoreType.DMA
    VMEM = pltpu.VMEM

    def body(inputs, out_grad, up_blocks, up_index, down_blocks, down_index):
        tokens, width = inputs.shape
        blocks = nr * KR
        hidden = NC * BLK
        share = CAP // nd
        vmem = pl.BlockSpec(memory_space=pltpu.VMEM)
        smem = pl.BlockSpec(memory_space=pltpu.SMEM)
        hbm = pl.BlockSpec(memory_space=pltpu.HBM)
        scratch = [
            VMEM((blocks * BLK // HALF, HALF, tokens), BF),
            VMEM((blocks * BLK // HALF, HALF, tokens), BF),
            VMEM((nr * CAP + 1, BLK, BLK), BF),
            VMEM((nr * CAP + 1, BLK, BLK), BF),
            VMEM((nr, 8, BLK), jnp.int32),
            pltpu.SMEM((nr, 8, BLK), jnp.int32),
            VMEM((tokens, hidden), F32),
            VMEM((hidden, tokens), F32),
            VMEM((hidden, tokens), F32),
            VMEM((NC, BLK, tokens), BF),
            VMEM((NC, BLK, tokens), BF),
            VMEM((nr, nd, share // 2, BLK, BLK), BF),
            VMEM((nd, nr, share // 2, BLK, BLK), BF),
            VMEM((nr, nd, share // 2, BLK, BLK), BF),
            VMEM((nd, nr, share // 2, BLK, BLK), BF),
            VMEM((2, 2, 2, 2, share // 2, BLK, BLK), BF),
            VMEM((2, 2, 2, 2, share // 2, BLK, BLK), BF),
            VMEM((2, 2, 2, 2, 2, share // 2, BLK, BLK), BF),
            VMEM((2, 2, 4, share // 2, BLK, BLK), BF),
            VMEM((2, 2, 3, share // 2, BLK, BLK), BF),
            VMEM((nz, 2, width, tokens), F32),
            VMEM((nz, width, tokens), BF),
            VMEM((nz, width, tokens), BF),
            VMEM((nz - 1, width, tokens), BF),
            VMEM((2, nz // 2, width, tokens), BF),
            VMEM((2, nz // 2, width, tokens), BF),
            DMA((2,)),
            DMA((nr,)), DMA((nr,)), DMA,
            DMA((2,)), DMA((2, nr)), DMA((2,)), DMA((2,)),
            DMA((2,)), DMA((2, 2, nz // 2)),
            DMA((2,)), DMA((nz,)), DMA,
            DMA((2, 2)), DMA((2, 2, 2)), DMA((2, 2, 2, 2)),
            DMA((2, 2)), DMA((2, 2, 3)),
            DMA, DMA((nz,)),
            DMA, DMA((2, nz // 2)), DMA((2, nz // 2)),
        ]
        def units(array):
            return array.T.reshape(width // HALF, HALF, tokens)

        in_grad, up_grad, down_grad = pl.pallas_call(
            functools.partial(kernel, (nd, nr, nz)),
            out_shape=(
                jax.ShapeDtypeStruct((width, tokens), BF),
                jax.ShapeDtypeStruct((1, 1, share, BLK, BLK), BF),
                jax.ShapeDtypeStruct((1, 1, share, BLK, BLK), BF),
            ),
            in_specs=[hbm, hbm, hbm, smem, hbm, smem],
            out_specs=(vmem, vmem, vmem),
            scratch_shapes=scratch,
            compiler_params=pltpu.CompilerParams(
                collective_id=0, has_side_effects=True, vmem_limit_bytes=60 << 20
            ),
        )(units(inputs), units(out_grad), up_blocks, up_index, down_blocks, down_index)
        return in_grad.T, up_grad, down_grad

    return jax.shard_map(
        body,
        mesh=mesh,
        in_specs=(
            P(("dp", "row"), "col"),
            P(("dp", "row"), "col"),
            P("row", "col", None, None, None),
            P("row", "col", None),
            P("row", "col", None, None, None),
            P("row", "col", None),
        ),
        out_specs=(
            P(("dp", "row"), "col"),
            P("row", "col", "dp", None, None),
            P("row", "col", "dp", None, None),
        ),
        check_vma=False,
    )
```

```python
import functools
import math

import jax
import jax.numpy as jnp
from jax import lax
from jax.experimental import pallas as pl
from jax.experimental.pallas import tpu as pltpu
from jax.sharding import PartitionSpec as P

MESH = pl.DeviceIdType.MESH
BF = jnp.bfloat16
F32 = jnp.float32
ROOT = math.sqrt(2.0 / math.pi)

BLK = 128
CAP = 16
KR = 12
NC = 6
HALF = 64
GATHER_TWOS = 3
PB = 3

DIRECT = (8, 4)


def tree(count, twos):
    strides = [2] * twos + [1] * (count - 2 * twos)
    marks = [0]
    for step in strides:
        marks.append(marks[-1] + step)
    return strides, marks


def gelu_parts(value):
    inner = ROOT * (value + 0.044715 * value * value * value)
    tanh_inner = jnp.tanh(inner)
    result = 0.5 * value * (1.0 + tanh_inner)
    slope = 0.5 * (1.0 + tanh_inner) + 0.5 * value * (
        1.0 - tanh_inner * tanh_inner
    ) * ROOT * (1.0 + 3.0 * 0.044715 * value * value)
    return result, slope


def nt_dot(a, b):
    return lax.dot_general(a, b, (((1,), (1,)), ((), ())), preferred_element_type=F32)


def kernel(
    sizes,
    x_hbm, g_hbm, wu_hbm, ui_ref, wd_hbm, di_ref,
    in_ref, up_ref, down_ref,
    xb, gb, wub, wdb, meta_v, meta_s, p_ref, a_ref, s_ref, pg_t, act_t,
    dw00, dw01, dw10, dw11, relay_in, relayed, one_in, half_sum, two_in,
    own, mine, theirs, ring_out, ring_leaf, ring_bone,
    first_l, meta_ss, meta_r, meta_l, wsend, whelp, wrecv, wlocal,
    ag_s, ag_r, sib_s, sib_r, sib_all,
    one_s, relay_r, one_r, two_s, two_r,
    part_s, part_r, ring_s, leaf_r, bone_r,
):
    nd, nr, nz = sizes
    tokens = BLK
    third = x_hbm.shape[0]
    width = third * HALF
    wide = 2 * third
    scale = 1.0 / math.sqrt(nd * nr * tokens)
    xg, wb = (xb, gb), (wub, wdb)
    dw = ((dw00, dw01), (dw10, dw11))
    d, r, c = lax.axis_index("dp"), lax.axis_index("row"), lax.axis_index("col")
    z, h = c // 2, c % 2
    sibling = (d, r, z * 2 + 1 - h)
    n_of = {1: nz // 2, -1: nz // 2 - 1}

    def xpeer(k):
        return (d, lax.rem(r + k, nr), c)

    def ypeer(k):
        return (lax.rem(d + k, nd), r, c)

    def zpeer(k):
        return (d, r, lax.rem(z + nz + k, nz) * 2 + h)

    def send(src, dst, ss, rs, to):
        copy = pltpu.make_async_remote_copy(
            src_ref=src, dst_ref=dst, send_sem=ss, recv_sem=rs, device_id=to, device_id_type=MESH
        )
        copy.start()

    def drain(ref, sem):
        pltpu.make_async_copy(ref, ref, sem).wait()

    own_rows = pl.ds(third * c, third)
    srcs = (x_hbm, g_hbm)
    firsts = [pltpu.make_async_copy(srcs[a], xg[a].at[own_rows], first_l.at[a]) for a in range(2)]
    srcw = (wu_hbm.at[0, 0], wd_hbm.at[0, 0])
    locals_ = [
        pltpu.make_async_copy(srcw[a], wb[a].at[pl.ds(CAP * r, CAP)], wlocal.at[a]) for a in range(2)
    ]
    for copy in firsts + locals_:
        copy.start()

    partners = [sibling] + [zpeer(k) for k in (1, -1, 2, -2)]
    partners += [xpeer(k) for k in range(1, nr)] + [ypeer(k) for k in range(1, nd)]
    barrier = pltpu.get_barrier_semaphore()
    for to in partners:
        pl.semaphore_signal(barrier, inc=1, device_id=to, device_id_type=MESH)

    pl.semaphore_wait(barrier, len(partners))

    def piece(a, k, core):
        where = lax.rem(z + nz + k, nz)
        return xg[a].at[pl.ds(wide * where + third * core, third)]

    def share(a, way, at):
        ref = piece(a, -way * at, h)
        arrived = sib_r.at[2 * at - 1 if way == 1 else 2 * at] if a == 0 else sib_all
        send(ref, ref, sib_s.at[a], arrived, sibling)

    trees = {way: tree(n_of[way], min(GATHER_TWOS, n_of[way] // 2)) for way in (1, -1)}

    def gather_send(a, way, at, hop):
        ref = piece(a, -way * at, h)
        side = 0 if way == 1 else 1
        send(ref, ref, ag_s.at[a], ag_r.at[a, side, at + hop - 1], zpeer(way * hop))

    def gather_wait(a, way, at):
        side = 0 if way == 1 else 1
        drain(piece(a, -way * at, h), ag_r.at[a, side, at - 1])

    def gather_step(a, way, j):
        strides, marks = trees[way]
        if j > len(strides):
            return
        at = marks[j]
        if j > 0:
            gather_wait(a, way, at)
        if j < len(strides):
            gather_send(a, way, at, strides[j])
            if strides[j] == 2:
                gather_send(a, way, at, 1)
        if j > 0:
            share(a, way, at)

    def gather_leaf(a, way, j):
        strides, marks = trees[way]
        if 0 < j <= len(strides) and strides[j - 1] == 2:
            gather_wait(a, way, marks[j] - 1)
            share(a, way, marks[j] - 1)

    for a in range(2):
        firsts[a].wait()
        for way in (1, -1):
            gather_step(a, way, 0)
    for a in range(2):
        share(a, -1, 0)

    per = [(CAP - direct) // nd for direct in DIRECT]

    def weights_help(a):
        for k in range(1, nr):
            send(
                srcw[a].at[pl.ds(per[a] * d, per[a])], wb[a].at[pl.ds(CAP * r + per[a] * d, per[a])],
                wsend.at[a], whelp.at[a, k], xpeer(k),
            )

    def weights_direct(a):
        for k in range(1, nr):
            send(
                srcw[a].at[pl.ds(CAP - DIRECT[a], DIRECT[a])],
                wb[a].at[pl.ds(CAP * r + CAP - DIRECT[a], DIRECT[a])],
                wsend.at[a], wrecv.at[a], xpeer(k),
            )

    weights_help(0)
    weights_help(1)
    weights_direct(0)

    lane = lax.broadcasted_iota(jnp.int32, (8, BLK), 1)
    line = lax.broadcasted_iota(jnp.int32, (8, BLK), 0)

    def publish():
        table = jnp.where(line >= 6, nr * CAP, 0)
        for s in range(CAP):
            up = ui_ref[0, 0, s]
            down = di_ref[0, 0, s]
            up_ok, down_ok = up >= 0, down >= 0
            up_p, down_p = jnp.maximum(up, 0), jnp.maximum(down, 0)
            entries = (
                r * KR + up_p // NC, up_p % NC, up_ok.astype(jnp.int32),
                down_p // KR, r * KR + down_p % KR, down_ok.astype(jnp.int32),
            )
            for i, entry in enumerate(entries):
                table = jnp.where((line == i) & (lane == s), entry, table)
            table = jnp.where((line == 6) & (lane == up), r * CAP + s, table)
            table = jnp.where((line == 7) & (lane == down), r * CAP + s, table)
        meta_v[r] = table
        for k in range(1, nr):
            send(meta_v.at[r], meta_v.at[r], meta_ss.at[k], meta_r.at[k], xpeer(k))
        for a in range(2):
            wb[a][nr * CAP] = jnp.zeros((BLK, BLK), BF)

    def help_on(a):
        for k in range(1, nr):
            src = lax.rem(r + nr - k, nr)
            ref = wb[a].at[pl.ds(CAP * src + per[a] * d, per[a])]
            drain(ref, whelp.at[a, k])
            for ky in range(1, nd):
                send(ref, ref, wsend.at[a], wrecv.at[a], ypeer(ky))

    sum_trees = {way: tree(n_of[way], n_of[way] // 2) for way in (1, -1)}

    weights_direct(1)
    publish()
    p_ref[...] = jnp.zeros_like(p_ref)
    a_ref[...] = jnp.zeros_like(a_ref)

    def tables():
        for k in range(1, nr):
            src = lax.rem(r + nr - k, nr)
            drain(meta_v.at[src], meta_r.at[k])
        to_smem = pltpu.make_async_copy(meta_v, meta_s, meta_l)
        to_smem.start()
        to_smem.wait()

    def weights_here(a):
        locals_[a].wait()
        got = (nr - 1) * DIRECT[a] + (nr - 1) * (nd - 1) * per[a]
        drain(wb[a].at[pl.ds(0, got)], wrecv.at[a])

    def forward():
        for i in range(nz):
            at = (i + 1) // 2
            where = lax.rem(z + nz + at * (1 - 2 * (i % 2)), nz)
            drain(xb.at[pl.ds(wide * where + third * (1 - h), third)], sib_r.at[i])

        @pl.loop(0, nr)
        def _(owner):
            deep = KR * BLK
            left = xb[pl.ds(2 * KR * owner, 2 * KR)].reshape(deep, tokens).T
            right = jnp.concatenate(
                [
                    jnp.concatenate([wub[meta_s[owner, 6, i * NC + j]] for j in range(NC)], axis=1)
                    for i in range(KR)
                ],
                axis=0,
            )
            p_ref[...] += jnp.dot(left, right, preferred_element_type=F32)

    longest = max(len(trees[way][0]) for way in (1, -1))
    for j in range(1, longest + 1):
        for a in range(2):
            for way in (1, -1):
                gather_step(a, way, j)
        for a in range(2):
            for way in (1, -1):
                gather_leaf(a, way, j)
        if j <= 2:
            help_on(j - 1)
    tables()
    weights_here(0)
    forward()
    drain(xg[1].at[pl.ds(0, third * nz)], sib_all)

    step_rows = 12
    steps = nr * KR // step_rows
    per_owner = KR // step_rows
    deep = step_rows * BLK

    act, slope = gelu_parts(p_ref[...])
    act_low = act.astype(BF)
    for i in range(NC):
        act_t[i] = act_low[:, i * BLK:(i + 1) * BLK].T
        s_ref[pl.ds(i * BLK, BLK), :] = slope[:, i * BLK:(i + 1) * BLK].T

    def block_rows(ref, k):
        return jnp.concatenate([ref[2 * k], ref[2 * k + 1]], axis=0)

    ways = ((r, nr, xpeer), (d, nd, ypeer))
    share_y = CAP // nd
    part = share_y // 2

    def terms(a, e, k):
        place, count, _ = ways[e]
        first = lax.rem(place + k, count)

        @pl.loop(0, ways[1 - e][1], unroll=4)
        def _(second):
            owner, owner_y = (first, second) if e == 0 else (second, first)
            for u in range(part):
                s = share_y * owner_y + part * e + u
                if a == 0:
                    i, j = meta_s[owner, 3, s], meta_s[owner, 4, s]
                    keep = meta_s[owner, 5, s].astype(F32) * scale
                    term = nt_dot(act_t[i], block_rows(gb, j))
                else:
                    i, j = meta_s[owner, 0, s], meta_s[owner, 1, s]
                    keep = meta_s[owner, 2, s].astype(F32) * scale
                    term = nt_dot(block_rows(xb, i), pg_t[j])
                dw[a][e][k, second, u] = (term * keep).astype(BF)

    def halves(a, e, k, side):
        return dw[a][e].at[k, pl.ds(2 * side, 2)]

    def relay_out(a, e):
        for side, k in ((0, 1), (1, 3)):
            send(halves(a, e, 2, side), relay_in.at[a, e, side], one_s.at[a, e], relay_r.at[a, e, side], ways[e][2](k))

    def direct_out(a, e, k):
        side = 1 if k == 1 else 0
        send(halves(a, e, k, side), one_in.at[a, e, k // 2, side], one_s.at[a, e], one_r.at[a, e, k // 2, side], ways[e][2](k))

    def relay_on(a, e):
        for side, k in ((0, 1), (1, 3)):
            drain(relay_in.at[a, e, side], relay_r.at[a, e, side])

            @pl.loop(0, 2)
            def _(t):
                for u in range(part):
                    total = dw[a][e][k, 2 * side + t, u].astype(F32) + relay_in[a, e, side, t, u].astype(F32)
                    relayed[a, e, side, t, u] = total.astype(BF)

            send(
                relayed.at[a, e, side], one_in.at[a, e, k // 2, side], one_s.at[a, e],
                one_r.at[a, e, k // 2, side], ways[e][2](k),
            )

    def second_out(a, e):
        for k in range(2):
            for side in range(2):
                drain(one_in.at[a, e, k, side], one_r.at[a, e, k, side])

        @pl.loop(0, 2)
        def _(t):
            for side in range(2):
                for u in range(part):
                    total = dw[a][e][0, 2 * side + t, u].astype(F32)
                    for k in range(2):
                        total += one_in[a, e, k, side, t, u].astype(F32)
                    half_sum[a, e, 2 * side + t, u] = total.astype(BF)

        place, count, peer = ways[1 - e]
        for k in (2, 1, 3):
            to = lax.rem(place + k, count)
            send(half_sum.at[a, e, to], two_in.at[a, e, k - 1], two_s.at[a, e], two_r.at[a, e, k - 1], peer(k))

    def finish(a, e):
        place, count, _ = ways[1 - e]
        for k in range(count - 1):
            drain(two_in.at[a, e, k], two_r.at[a, e, k])
        out = (down_ref, up_ref)[a]
        for u in range(part):
            total = half_sum[a, e, place, u].astype(F32)
            for k in range(count - 1):
                total += two_in[a, e, k, u].astype(F32)
            out[0, 0, part * e + u] = total.astype(BF)

    def act_gradient():
        weights_here(1)

        @pl.loop(0, steps)
        def _(t):
            owner, base = t // per_owner, (t % per_owner) * step_rows
            right = gb[pl.ds(2 * step_rows * t, 2 * step_rows)].reshape(deep, tokens)
            left = jnp.concatenate(
                [
                    jnp.concatenate(
                        [wdb[meta_s[owner, 7, i * KR + base + j]] for j in range(step_rows)], axis=1
                    )
                    for i in range(NC)
                ],
                axis=0,
            )
            a_ref[...] += jnp.dot(left, right, preferred_element_type=F32)

        for i in range(NC):
            rows = pl.ds(i * BLK, BLK)
            pg_t[i] = (a_ref[rows, :] * s_ref[rows, :]).astype(BF)

    def partial_piece(index, k):
        partial_store(index, partial_dot(k))

    def partial_dot(k):
        where = lax.rem(z + nz + k, nz)
        owner = where // (KR // PB)
        base = (where % (KR // PB)) * PB
        left = jnp.concatenate(
            [
                jnp.concatenate(
                    [wub[meta_s[owner, 6, (base + i) * NC + j]] for j in range(NC)], axis=1
                )
                for i in range(PB)
            ],
            axis=0,
        )
        right = jnp.concatenate([pg_t[j] for j in range(NC)], axis=0)
        return jnp.dot(left, right, preferred_element_type=F32)

    def partial_store(index, both):
        own[index] = both.reshape(2, width, tokens)
        mine[index] = own[index, 1 - h].astype(BF)
        send(mine.at[index], theirs.at[index], part_s, part_r.at[index], sibling)

    n_right, n_left = n_of[1], n_of[-1]

    def index_of(way, at):
        return at - 1 if way == 1 else n_right + at - 1

    order = []
    for at in range(n_right, 0, -1):
        order.append((1, at))
        if at <= n_left:
            order.append((-1, at))
    def summed(index, extra):
        drain(theirs.at[index], part_r.at[index])
        total = own[index, h] + theirs[index].astype(F32)
        for ref in extra:
            total = total + ref[...].astype(F32)
        return total

    def incoming(way, at):
        strides, marks = sum_trees[way]
        side = 0 if way == 1 else 1
        refs = []
        j = marks.index(at)
        if j < len(strides):
            if strides[j] == 2:
                refs.append((ring_leaf.at[side, at], leaf_r.at[side, at]))
            refs.append((ring_bone.at[side, at], bone_r.at[side, at]))
        return refs

    def ring_step(way, at):
        strides, marks = sum_trees[way]
        side = 0 if way == 1 else 1
        index = index_of(way, at)
        ref = ring_out.at[index]
        if at in marks:
            pairs = incoming(way, at)
            for more, sem in pairs:
                drain(more, sem)
            hop = strides[marks.index(at) - 1]
            ref[...] = summed(index, [more for more, _ in pairs]).astype(BF)
            send(ref, ring_bone.at[side, at - hop], ring_s, bone_r.at[side, at - hop], zpeer(way * hop))
        else:
            ref[...] = summed(index, []).astype(BF)
            send(ref, ring_leaf.at[side, at - 1], ring_s, leaf_r.at[side, at - 1], zpeer(way))

    def waits(way, at):
        return at in sum_trees[way][1][:-1]

    def ring_chain(level):
        for way in (1, -1):
            inner = sum_trees[way][1][1:-1][::-1]
            if level < len(inner):
                ring_step(way, inner[level])

    def ring_end():
        pairs = incoming(1, 0) + incoming(-1, 0)
        for ref, sem in pairs:
            drain(ref, sem)
        in_ref[...] = summed(nz - 1, [ref for ref, _ in pairs]).astype(BF)

    for e in (0, 1):
        terms(0, e, 2)
        relay_out(0, e)
    act_gradient()
    for e in (0, 1):
        terms(1, e, 2)
        relay_out(1, e)
    before = []
    for at in range(n_right, 0, -1):
        both = [(way, at) for way in (1, -1) if at <= n_of[way]]
        dots = [partial_dot(way * at) for way, at in both]
        for (way, at), value in zip(both, dots):
            partial_store(index_of(way, at), value)
        for one in before:
            if not waits(*one):
                ring_step(*one)
        before = both
    for one in before:
        if not waits(*one):
            ring_step(*one)
    for a in (0, 1):
        for e in (0, 1):
            for k in (1, 3):
                terms(a, e, k)
                direct_out(a, e, k)
        if a == 0:
            ring_chain(0)
            for e in (0, 1):
                relay_on(a, e)
    ring_chain(1)
    partial_piece(nz - 1, 0)
    for e in (0, 1):
        relay_on(1, e)
    for a in (0, 1):
        for e in (0, 1):
            terms(a, e, 0)
    ring_chain(2)
    for e in (0, 1):
        second_out(0, e)
    ring_end()
    for e in (0, 1):
        second_out(1, e)
    for a in (0, 1):
        for e in (0, 1):
            finish(a, e)

    for a in range(2):
        drain(xg[a].at[pl.ds(0, third * (nz - 1))], ag_s.at[a])
        drain(xg[a].at[pl.ds(0, third * nz)], sib_s.at[a])
        gone = (nr - 1) * (per[a] + DIRECT[a]) + (nr - 1) * (nd - 1) * per[a]
        drain(wb[a].at[pl.ds(0, gone)], wsend.at[a])
    for k in range(1, nr):
        drain(meta_v.at[r], meta_ss.at[k])
    for a in range(2):
        for e in range(2):
            for _ in range(3):
                drain(relay_in.at[a, e], one_s.at[a, e])
            drain(two_in.at[a, e], two_s.at[a, e])

    drain(mine, part_s)
    drain(ring_out, ring_s)


def solution(mesh):
    nd, nr, nc = mesh.shape["dp"], mesh.shape["row"], mesh.shape["col"]
    nz = nc // 2
    DMA = pltpu.SemaphoreType.DMA
    VMEM = pltpu.VMEM

    def body(inputs, out_grad, up_blocks, up_index, down_blocks, down_index):
        tokens, width = inputs.shape
        blocks = nr * KR
        hidden = NC * BLK
        share = CAP // nd
        vmem = pl.BlockSpec(memory_space=pltpu.VMEM)
        smem = pl.BlockSpec(memory_space=pltpu.SMEM)
        hbm = pl.BlockSpec(memory_space=pltpu.HBM)
        scratch = [
            VMEM((blocks * BLK // HALF, HALF, tokens), BF),
            VMEM((blocks * BLK // HALF, HALF, tokens), BF),
            VMEM((nr * CAP + 1, BLK, BLK), BF),
            VMEM((nr * CAP + 1, BLK, BLK), BF),
            VMEM((nr, 8, BLK), jnp.int32),
            pltpu.SMEM((nr, 8, BLK), jnp.int32),
            VMEM((tokens, hidden), F32),
            VMEM((hidden, tokens), F32),
            VMEM((hidden, tokens), F32),
            VMEM((NC, BLK, tokens), BF),
            VMEM((NC, BLK, tokens), BF),
            VMEM((nr, nd, share // 2, BLK, BLK), BF),
            VMEM((nd, nr, share // 2, BLK, BLK), BF),
            VMEM((nr, nd, share // 2, BLK, BLK), BF),
            VMEM((nd, nr, share // 2, BLK, BLK), BF),
            VMEM((2, 2, 2, 2, share // 2, BLK, BLK), BF),
            VMEM((2, 2, 2, 2, share // 2, BLK, BLK), BF),
            VMEM((2, 2, 2, 2, 2, share // 2, BLK, BLK), BF),
            VMEM((2, 2, 4, share // 2, BLK, BLK), BF),
            VMEM((2, 2, 3, share // 2, BLK, BLK), BF),
            VMEM((nz, 2, width, tokens), F32),
            VMEM((nz, width, tokens), BF),
            VMEM((nz, width, tokens), BF),
            VMEM((nz - 1, width, tokens), BF),
            VMEM((2, nz // 2, width, tokens), BF),
            VMEM((2, nz // 2, width, tokens), BF),
            DMA((2,)),
            DMA((nr,)), DMA((nr,)), DMA,
            DMA((2,)), DMA((2, nr)), DMA((2,)), DMA((2,)),
            DMA((2,)), DMA((2, 2, nz // 2)),
            DMA((2,)), DMA((nz,)), DMA,
            DMA((2, 2)), DMA((2, 2, 2)), DMA((2, 2, 2, 2)),
            DMA((2, 2)), DMA((2, 2, 3)),
            DMA, DMA((nz,)),
            DMA, DMA((2, nz // 2)), DMA((2, nz // 2)),
        ]
        def units(array):
            return array.T.reshape(width // HALF, HALF, tokens)

        in_grad, up_grad, down_grad = pl.pallas_call(
            functools.partial(kernel, (nd, nr, nz)),
            out_shape=(
                jax.ShapeDtypeStruct((width, tokens), BF),
                jax.ShapeDtypeStruct((1, 1, share, BLK, BLK), BF),
                jax.ShapeDtypeStruct((1, 1, share, BLK, BLK), BF),
            ),
            in_specs=[hbm, hbm, hbm, smem, hbm, smem],
            out_specs=(vmem, vmem, vmem),
            scratch_shapes=scratch,
            compiler_params=pltpu.CompilerParams(
                collective_id=0, has_side_effects=True, vmem_limit_bytes=60 << 20
            ),
        )(units(inputs), units(out_grad), up_blocks, up_index, down_blocks, down_index)
        return in_grad.T, up_grad, down_grad

    return jax.shard_map(
        body,
        mesh=mesh,
        in_specs=(
            P(("dp", "row"), "col"),
            P(("dp", "row"), "col"),
            P("row", "col", None, None, None),
            P("row", "col", None),
            P("row", "col", None, None, None),
            P("row", "col", None),
        ),
        out_specs=(
            P(("dp", "row"), "col"),
            P("row", "col", "dp", None, None),
            P("row", "col", "dp", None, None),
        ),
        check_vma=False,
    )
```
